256 devices in a mesh: seq: 64 (over z, x, y_lo), chan: 4 (over y_hi, core).
Axes of the slice: x: 4, y: 4 (y_hi: 2, y_lo: 2; y = y_hi * 2 + y_lo), z: 8, core: 2. Of those that a mesh axis runs over, the one named last changes fastest.
Arguments:
- query_input: bfloat16 [256, 32768], P('chan', 'seq'), may hold values from -6 to 6
- key_input: bfloat16 [256, 32768], P('chan', 'seq'), may hold values from -6 to 6
- value_input: bfloat16 [256, 32768], P('chan', 'seq'), may hold values from -6 to 6
- long_filter: float32 [64, 32768], P('chan', 'seq'), may hold values from -3 to 3
- query_taps: float32 [3, 256], P(None, 'chan'), may hold values from -3 to 3
- key_taps: float32 [3, 256], P(None, 'chan'), may hold values from -3 to 3
- value_taps: float32 [3, 256], P(None, 'chan'), may hold values from -3 to 3
- skip_gain: float32 [256], P('chan'), may hold values from -3 to 3
- out_cotangent: bfloat16 [256, 32768], P('chan', 'seq'), may hold values from -6 to 6
Outputs:
- gated_output: bfloat16 [256, 32768], P('chan', 'seq')
- query_gradient: bfloat16 [256, 32768], P('chan', 'seq')
- key_gradient: bfloat16 [256, 32768], P('chan', 'seq')
- value_gradient: bfloat16 [256, 32768], P('chan', 'seq')
The draws below stay inside these ranges and needn't reach their ends.
All inputs are finite; a program needn't handle non-finite values.
Results may differ from the reference program's by a relative error of at most 0.00175.
Values may be sent and summed in bfloat16 or wider, within the bound.
A program may use at most 128 MiB of HBM per device.

```python
import math
import jax
import jax.numpy as jnp

FILTER_TOTAL = 64
CHANNELS = 256
SEQUENCE_LENGTH = 32768


def draw_long_filter(key, part):
    key = jax.random.fold_in(key, 17)
    random_keys = jax.random.split(key, 7)
    position_grid = jnp.arange(SEQUENCE_LENGTH, dtype=jnp.float32)[None, :]
    decay_rates = jnp.exp(jax.random.uniform(random_keys[0], (FILTER_TOTAL, 1), minval=math.log(0.5 / SEQUENCE_LENGTH), maxval=math.log(1.0 / 30.0)))
    noise_part = jax.random.truncated_normal(random_keys[4], -4.0, 4.0, (FILTER_TOTAL, SEQUENCE_LENGTH))
    spike_positions = jax.random.randint(random_keys[5], (FILTER_TOTAL, 3), 0, SEQUENCE_LENGTH).astype(jnp.float32)
    spike_mask = jax.random.uniform(random_keys[6], (FILTER_TOTAL, 3), minval=0.5, maxval=0.8)
    amplitude = jnp.sqrt(2.0 * decay_rates / -jnp.expm1(-2.0 * decay_rates * SEQUENCE_LENGTH))
    decay_window = jnp.exp(-decay_rates * position_grid) * amplitude
    for spike_index in range(3):
        decay_window = decay_window * jnp.where(position_grid >= spike_positions[:, spike_index:spike_index + 1], spike_mask[:, spike_index:spike_index + 1], 1.0)
    return (decay_window * noise_part).astype(jnp.float32)


def levels(key, shape, cuts, smallest, high):
    factor_of = 1.0
    for axis_at, blocks in cuts:
        steps = jax.random.uniform(jax.random.fold_in(jax.random.fold_in(key, 6), axis_at), (blocks,), jnp.float32, smallest / len(cuts), high / len(cuts))
        factor_of = factor_of * jnp.repeat(jnp.exp(steps), shape[axis_at] // blocks).reshape((-1,) + (1,) * (len(shape) - 1 - axis_at))
    return factor_of


def normal_values(key, extent, width, bound, shards=(), held_as=jnp.bfloat16):
    array = jax.random.normal(key, extent, jnp.float32) * width
    if len(shards) > 0:
        array = levels(key, extent, shards, -0.22, 0.18) * array
    return jnp.clip(array, min=-bound, max=bound).astype(held_as)


def setup_inputs(seed: int = 0) -> dict:
    key_list = jax.random.split(jax.random.key(seed), 10)
    query_input = normal_values(key_list[0], (CHANNELS, SEQUENCE_LENGTH), 1.0, 6.0, ((0, 4), (1, 64)))
    key_input = normal_values(key_list[1], (CHANNELS, SEQUENCE_LENGTH), 1.0, 6.0, ((0, 4), (1, 64)))
    value_input = normal_values(key_list[2], (CHANNELS, SEQUENCE_LENGTH), 1.0, 6.0, ((0, 4), (1, 64)))
    long_filter = draw_long_filter(jax.random.fold_in(key_list[9], 71), 0)
    query_taps = normal_values(key_list[4], (3, CHANNELS), 0.6, 3.0, ((1, 4),), jnp.float32)
    key_taps = normal_values(key_list[5], (3, CHANNELS), 0.6, 3.0, ((1, 4),), jnp.float32)
    value_taps = normal_values(key_list[6], (3, CHANNELS), 0.6, 3.0, ((1, 4),), jnp.float32)
    skip_gain = normal_values(key_list[7], (CHANNELS,), 0.5, 3.0, ((0, 4),), jnp.float32)
    out_cotangent = normal_values(key_list[8], (CHANNELS, SEQUENCE_LENGTH), 1.0, 6.0, ((0, 4), (1, 64)))
    return {"query_input": query_input, "key_input": key_input, "value_input": value_input, "long_filter": long_filter, "query_taps": query_taps, "key_taps": key_taps, "value_taps": value_taps, "skip_gain": skip_gain, "out_cotangent": out_cotangent}


def causal_short(signal, taps):
    padded = jnp.pad(signal, ((0, 0), (2, 0)))
    return taps[0][:, None] * signal + taps[1][:, None] * padded[:, 1:-1] + taps[2][:, None] * padded[:, :-2]


def reverse_short(signal, taps):
    padded = jnp.pad(signal, ((0, 0), (0, 2)))
    return taps[0][:, None] * signal + taps[1][:, None] * padded[:, 1:-1] + taps[2][:, None] * padded[:, 2:]


def reference(query_input, key_input, value_input, long_filter, query_taps, key_taps, value_taps, skip_gain, out_cotangent):
    short_q = causal_short(query_input.astype(jnp.float32), query_taps)
    short_k = causal_short(key_input.astype(jnp.float32), key_taps)
    short_v = causal_short(value_input.astype(jnp.float32), value_taps)
    product = short_k * short_v
    filters = jnp.tile(long_filter, (CHANNELS // FILTER_TOTAL, 1))
    full_len = 2 * SEQUENCE_LENGTH
    filter_spec = jnp.fft.rfft(filters, n=full_len, axis=1)
    causal = jnp.fft.irfft(filter_spec * jnp.fft.rfft(product, n=full_len, axis=1), n=full_len, axis=1)[:, :SEQUENCE_LENGTH]
    skip_col = skip_gain[:, None]
    mixed = causal + skip_col * product
    gated_output = (short_q * mixed).astype(jnp.bfloat16)
    cotangent = out_cotangent.astype(jnp.float32)
    grad_mixed = cotangent * short_q
    grad_short_q = cotangent * mixed
    backward = jnp.fft.irfft(jnp.conj(filter_spec) * jnp.fft.rfft(grad_mixed, n=full_len, axis=1), n=full_len, axis=1)[:, :SEQUENCE_LENGTH]
    grad_product = backward + skip_col * grad_mixed
    grad_short_k = grad_product * short_v
    grad_short_v = grad_product * short_k
    query_gradient = reverse_short(grad_short_q, query_taps).astype(jnp.bfloat16)
    key_gradient = reverse_short(grad_short_k, key_taps).astype(jnp.bfloat16)
    value_gradient = reverse_short(grad_short_v, value_taps).astype(jnp.bfloat16)
    return gated_output, query_gradient, key_gradient, value_gradient
```

```python
import functools

import jax
import jax.numpy as jnp
import ml_dtypes
import numpy as np
from jax import lax
from jax.experimental import pallas as pl
from jax.experimental.pallas import tpu as pltpu
from jax.sharding import PartitionSpec as P

SEQ = 64
CHAN = 4
BLOCK = 512
LANES = 128
ROWS = 256
FILTERS = SEQ // CHAN
FULL = 2 * ROWS * LANES

BF16 = jnp.bfloat16
F32 = jnp.float32
MESH = pl.DeviceIdType.MESH


def split_table(table):
    high = table.astype(ml_dtypes.bfloat16)
    low = (table - high.astype(np.float64)).astype(ml_dtypes.bfloat16)
    return high, low


@functools.lru_cache(maxsize=None)
def tables():
    k1 = np.arange(ROWS)
    a = np.arange(ROWS)
    b = np.arange(LANES)
    outer = 2 * np.pi * ((a[None, :] * (2 * k1[:, None] + 1)) % 1024) / 1024.0
    first = np.concatenate([np.cos(outer), -np.sin(outer)], axis=0)
    last = first.T * (2.0 / FULL)
    twist = 2 * np.pi * (b[None, :] * (2 * k1[:, None] + 1)) / (2.0 * FULL)
    inner = 2 * np.pi * ((b[None, :] * b[:, None]) % LANES) / LANES
    cosine, sine = np.cos(inner), np.sin(inner)
    mid = np.block([[cosine, -sine], [sine, cosine]])
    back = np.block([[cosine, sine], [-sine, cosine]])
    first_h, first_l = split_table(first)
    last_h, last_l = split_table(last)
    mid_h, mid_l = split_table(mid)
    back_h, back_l = split_table(back)
    return (
        np.stack([first_h, first_l]),
        np.stack([last_h, last_l]),
        np.stack([mid_h, mid_l]),
        np.stack([back_h, back_l]),
        np.stack([np.cos(twist), np.sin(twist)]).astype(np.float32),
    )


def split(value):
    high = value.astype(BF16)
    low = (value - high.astype(F32)).astype(BF16)
    return high, low


def dot(left, right):
    return jnp.dot(left, right, preferred_element_type=F32)


def table_left(table, high, low):
    table_h, table_l = table[0], table[1]
    left = jnp.concatenate([table_h, table_h, table_l], axis=1)
    return dot(left, jnp.concatenate([high, low, high], axis=0))


def table_right(high, low, table):
    table_h, table_l = table[0], table[1]
    right = jnp.concatenate([table_h, table_h, table_l], axis=0)
    return dot(jnp.concatenate([high, low, high], axis=1), right)


def swap_matrix():
    row = lax.broadcasted_iota(jnp.int32, (256, 256), 0)
    col = lax.broadcasted_iota(jnp.int32, (256, 256), 1)
    hit = (row % 16 == col // 16) & (row // 16 == col % 16)
    return jnp.where(hit, 1.0, 0.0).astype(BF16)


def sort_matrix(outer, kinds, to_kinds):
    size = outer * kinds * 4
    row = lax.broadcasted_iota(jnp.int32, (size, size), 0)
    col = lax.broadcasted_iota(jnp.int32, (size, size), 1)
    by_kind, by_shard = (row, col) if to_kinds else (col, row)
    kind = by_kind // (outer * 4)
    shard = (by_kind // 4) % outer
    hit = by_shard == shard * (kinds * 4) + kind * 4 + by_kind % 4
    return jnp.where(hit, 1.0, 0.0).astype(BF16)


def delayed(value, steps):
    lane = lax.broadcasted_iota(jnp.int32, (ROWS, LANES), 1)
    row = lax.broadcasted_iota(jnp.int32, (ROWS, LANES), 0)
    turned = pltpu.roll(value, steps, 1)
    above = jnp.where(row == 0, 0.0, pltpu.roll(turned, 1, 0))
    return jnp.where(lane < steps, above, turned)


def advanced(value, steps):
    lane = lax.broadcasted_iota(jnp.int32, (ROWS, LANES), 1)
    row = lax.broadcasted_iota(jnp.int32, (ROWS, LANES), 0)
    turned = pltpu.roll(value, LANES - steps, 1)
    below = jnp.where(row == ROWS - 1, 0.0, pltpu.roll(turned, ROWS - 1, 0))
    return jnp.where(lane >= LANES - steps, below, turned)


def kernel(
    q_ref, k_ref, v_ref, g_ref, filt_ref, qt_ref, kt_ref, vt_ref, gain_ref,
    first_hbm, last_hbm, mid_hbm, back_hbm, twist_hbm,
    oq_ref, dq_ref, dk_ref, dv_ref,
    first_ref, last_ref, mid_ref, back_ref, twist_ref,
    send_x, recv_x, send_f, recv_f, send_y, recv_y,
    table_sem, send_x_sem, recv_x_sem, send_f_sem, recv_f_sem,
    share_send_sem, share_recv_sem, send_y_sem, recv_y_sem,
):
    me = lax.axis_index("seq")
    group = lax.axis_index("chan")
    me_z, me_x, me_y = me // 8, (me // 2) % 4, me % 2

    def partner(step):
        dz = (step * 3) % 8
        dx = (step // 8) % 4
        dy = step // 32
        return ((me_z + dz) % 8) * 8 + ((me_x + dx) % 4) * 2 + (me_y + dy) % 2

    table_copies = [
        pltpu.make_async_copy(source, target, table_sem.at[index])
        for index, (source, target) in enumerate(
            [
                (first_hbm, first_ref),
                (mid_hbm, mid_ref),
                (twist_hbm, twist_ref),
                (back_hbm, back_ref),
                (last_hbm, last_ref),
            ]
        )
    ]

    barrier = pltpu.get_barrier_semaphore()

    def greet(step, carry):
        pl.semaphore_signal(barrier, inc=1, device_id={"seq": partner(step)}, device_id_type=MESH)
        return carry

    lax.fori_loop(1, SEQ, greet, 0)
    source_group = me // FILTERS

    def greet_source(step, carry):
        source = group * FILTERS + (me + step) % FILTERS

        @pl.when(jnp.logical_not((source == me) & (source_group == group)))
        def _():
            pl.semaphore_signal(
                barrier, inc=1, device_id={"seq": source, "chan": source_group}, device_id_type=MESH
            )

        return carry

    lax.fori_loop(0, FILTERS, greet_source, 0)
    for step in range(1, CHAN):
        pl.semaphore_signal(
            barrier, inc=1, device_id={"chan": (group + step) % CHAN}, device_id_type=MESH
        )
    for copy in table_copies:
        copy.start()

    filt_h, filt_l = split(filt_ref[...])
    pieces = [part[:, LANES * j : LANES * (j + 1)] for part in (filt_h, filt_l) for j in range(4)]
    row = lax.broadcasted_iota(jnp.int32, (128, 128), 0)
    col = lax.broadcasted_iota(jnp.int32, (128, 128), 1)
    regroup = jnp.where((row % 8 == col // 16) & (row // 8 == col % 16), 1.0, 0.0).astype(BF16)
    send_f[...] = dot(regroup, jnp.concatenate(pieces, axis=0)).astype(BF16).reshape(FILTERS, 8, LANES)
    swap = swap_matrix()
    for m in range(4):
        pieces = [
            ref[16 * m : 16 * (m + 1), LANES * j : LANES * (j + 1)]
            for ref in (q_ref, k_ref, v_ref, g_ref)
            for j in range(4)
        ]
        mixed_rows = dot(swap, jnp.concatenate(pieces, axis=0)).astype(BF16)
        send_x[16 * m : 16 * (m + 1)] = mixed_rows.reshape(16, 16, LANES)

    own_filter = (me // FILTERS == group) & (source_group == group)
    pl.semaphore_wait(barrier, SEQ - 1 + FILTERS + CHAN - 1 - own_filter.astype(jnp.int32))

    def send_filter(step, carry):
        r = (me + step) % FILTERS
        target = group * FILTERS + r
        to_self = (target == me) & (source_group == group)

        @pl.when(to_self)
        def _():
            pltpu.make_async_copy(send_f.at[r], recv_f.at[me], recv_f_sem).start()

        @pl.when(jnp.logical_not(to_self))
        def _():
            pltpu.make_async_remote_copy(
                src_ref=send_f.at[r],
                dst_ref=recv_f.at[me],
                send_sem=send_f_sem,
                recv_sem=recv_f_sem,
                device_id={"seq": target, "chan": source_group},
                device_id_type=MESH,
            ).start()

        return carry

    lax.fori_loop(0, FILTERS, send_filter, 0)

    pltpu.make_async_copy(send_x.at[me], recv_x.at[me], recv_x_sem).start()

    def send_inputs(step, carry):
        target = partner(step)
        pltpu.make_async_remote_copy(
            src_ref=send_x.at[target],
            dst_ref=recv_x.at[me],
            send_sem=send_x_sem,
            recv_sem=recv_x_sem,
            device_id={"seq": target},
            device_id_type=MESH,
        ).start()
        return carry

    lax.fori_loop(1, SEQ, send_inputs, 0)

    part = recv_f.at[pl.ds(group * FILTERS, FILTERS)]
    pltpu.make_async_copy(part, part, recv_f_sem).wait()
    for step in range(1, CHAN):
        pltpu.make_async_remote_copy(
            src_ref=part,
            dst_ref=part,
            send_sem=share_send_sem,
            recv_sem=share_recv_sem,
            device_id={"chan": (group + step) % CHAN},
            device_id_type=MESH,
        ).start()
    three = recv_f.at[pl.ds(0, (CHAN - 1) * FILTERS)]
    pltpu.make_async_copy(three, three, share_recv_sem).wait()

    sort_f = sort_matrix(32, 2, True)
    filt_hi, filt_lo = [], []
    for m in range(2):
        got = recv_f[32 * m : 32 * (m + 1)].reshape(256, LANES)
        rows = dot(sort_f, got).astype(BF16)
        filt_hi.append(rows[:128])
        filt_lo.append(rows[128:])

    for copy in table_copies:
        copy.wait()

    pltpu.make_async_copy(recv_x, recv_x, recv_x_sem).wait()
    sort_x = sort_matrix(16, 4, True)
    parts = []
    for m in range(4):
        got = recv_x[16 * m : 16 * (m + 1)].reshape(256, LANES)
        parts.append(dot(sort_x, got))
    query, key, value, cotangent = (
        jnp.concatenate([rows[64 * i : 64 * (i + 1)] for rows in parts], axis=0) for i in range(4)
    )

    def causal_taps(signal, taps):
        return (
            taps[0, me] * signal + taps[1, me] * delayed(signal, 1) + taps[2, me] * delayed(signal, 2)
        )

    def reverse_taps(signal, taps):
        return (
            taps[0, me] * signal + taps[1, me] * advanced(signal, 1) + taps[2, me] * advanced(signal, 2)
        )

    short_q = causal_taps(query, qt_ref)
    short_k = causal_taps(key, kt_ref)
    short_v = causal_taps(value, vt_ref)
    product = short_k * short_v
    grad_mixed = cotangent * short_q

    prod_h, prod_l = split(product)
    grad_h, grad_l = split(grad_mixed)
    high = jnp.concatenate([jnp.concatenate(filt_hi, axis=0), prod_h, grad_h], axis=1)
    low = jnp.concatenate([jnp.concatenate(filt_lo, axis=0), prod_l, grad_l], axis=1)
    outer = table_left(first_ref, high, low)
    cosine, sine = twist_ref[0], twist_ref[1]

    def spectrum(index):
        real = outer[:ROWS, LANES * index : LANES * (index + 1)]
        imag = outer[ROWS:, LANES * index : LANES * (index + 1)]
        turned = jnp.concatenate([real * cosine + imag * sine, imag * cosine - real * sine], axis=1)
        whole = table_right(*split(turned), mid_ref)
        return whole[:, :LANES], whole[:, LANES:]

    filt_re, filt_im = spectrum(0)

    def inverse(real, imag):
        back = table_right(*split(jnp.concatenate([real, imag], axis=1)), back_ref)
        real, imag = back[:, :LANES], back[:, LANES:]
        return jnp.concatenate([real * cosine - imag * sine, imag * cosine + real * sine], axis=0)

    prod_re, prod_im = spectrum(1)
    fwd = inverse(filt_re * prod_re - filt_im * prod_im, filt_re * prod_im + filt_im * prod_re)
    grad_re, grad_im = spectrum(2)
    bwd = inverse(filt_re * grad_re + filt_im * grad_im, filt_re * grad_im - filt_im * grad_re)
    both = table_left(last_ref, *split(jnp.concatenate([fwd, bwd], axis=1)))
    causal, backward = both[:, :LANES], both[:, LANES:]

    gain = gain_ref[me]
    mixed = causal + gain * product
    gated = short_q * mixed
    grad_product = backward + gain * grad_mixed
    outs = [
        gated.astype(BF16),
        reverse_taps(cotangent * mixed, qt_ref).astype(BF16),
        reverse_taps(grad_product * short_v, kt_ref).astype(BF16),
        reverse_taps(grad_product * short_k, vt_ref).astype(BF16),
    ]
    sort_y = sort_matrix(16, 4, False)
    for m in range(4):
        rows = jnp.concatenate([out[64 * m : 64 * (m + 1)] for out in outs], axis=0)
        send_y[16 * m : 16 * (m + 1)] = dot(sort_y, rows).astype(BF16).reshape(16, 16, LANES)

    pltpu.make_async_copy(send_y.at[me], recv_y.at[me], recv_y_sem).start()

    def send_outputs(step, carry):
        target = partner(step)
        pltpu.make_async_remote_copy(
            src_ref=send_y.at[target],
            dst_ref=recv_y.at[me],
            send_sem=send_y_sem,
            recv_sem=recv_y_sem,
            device_id={"seq": target},
            device_id_type=MESH,
        ).start()
        return carry

    lax.fori_loop(1, SEQ, send_outputs, 0)

    sent = send_x.at[pl.ds(0, SEQ - 1)]
    pltpu.make_async_copy(sent, sent, send_x_sem).wait()
    pltpu.make_async_copy(three, three, share_send_sem).wait()

    @pl.when(own_filter)
    def _():
        some = send_f.at[pl.ds(0, FILTERS - 1)]
        pltpu.make_async_copy(some, some, send_f_sem).wait()

    @pl.when(jnp.logical_not(own_filter))
    def _():
        pltpu.make_async_copy(send_f, send_f, send_f_sem).wait()

    pltpu.make_async_copy(recv_y, recv_y, recv_y_sem).wait()
    for m in range(4):
        rows = dot(swap, recv_y[16 * m : 16 * (m + 1)].reshape(256, LANES)).astype(BF16)
        for i, ref in enumerate((oq_ref, dq_ref, dk_ref, dv_ref)):
            for j in range(4):
                at = (4 * i + j) * 16
                ref[16 * m : 16 * (m + 1), LANES * j : LANES * (j + 1)] = rows[at : at + 16]
    sent = send_y.at[pl.ds(0, SEQ - 1)]
    pltpu.make_async_copy(sent, sent, send_y_sem).wait()


def body(q, k, v, long_filter, q_taps, k_taps, v_taps, gain, cotangent):
    constants = [jnp.asarray(table) for table in tables()]
    vmem = pl.BlockSpec(memory_space=pltpu.VMEM)
    smem = pl.BlockSpec(memory_space=pltpu.SMEM)
    anywhere = pl.BlockSpec(memory_space=pl.ANY)
    block = jax.ShapeDtypeStruct((SEQ, BLOCK), BF16)
    exchange = pltpu.VMEM((SEQ, 16, LANES), BF16)
    return pl.pallas_call(
        kernel,
        out_shape=[block] * 4,
        in_specs=[vmem] * 5 + [smem] * 4 + [anywhere] * 5,
        out_specs=[vmem] * 4,
        scratch_shapes=[
            pltpu.VMEM((2, 512, 256), BF16),
            pltpu.VMEM((2, 256, 512), BF16),
            pltpu.VMEM((2, 256, 256), BF16),
            pltpu.VMEM((2, 256, 256), BF16),
            pltpu.VMEM((2, ROWS, LANES), F32),
            exchange,
            exchange,
            pltpu.VMEM((FILTERS, 8, LANES), BF16),
            pltpu.VMEM((SEQ, 8, LANES), BF16),
            exchange,
            exchange,
            pltpu.SemaphoreType.DMA((5,)),
        ]
        + [pltpu.SemaphoreType.DMA] * 8,
        compiler_params=pltpu.CompilerParams(
            collective_id=0, has_side_effects=True, vmem_limit_bytes=40 * 1024 * 1024
        ),
        name="hyena",
    )(q, k, v, cotangent, long_filter, q_taps, k_taps, v_taps, gain, *constants)


def solution(mesh):
    in_specs = (
        P("chan", "seq"),
        P("chan", "seq"),
        P("chan", "seq"),
        P("chan", "seq"),
        P(None, "chan"),
        P(None, "chan"),
        P(None, "chan"),
        P("chan"),
        P("chan", "seq"),
    )
    out_specs = (P("chan", "seq"),) * 4
    return jax.shard_map(body, mesh=mesh, in_specs=in_specs, out_specs=out_specs, check_vma=False)
```

```python
import functools

import jax
import jax.numpy as jnp
import ml_dtypes
import numpy as np
from jax import lax
from jax.experimental import pallas as pl
from jax.experimental.pallas import tpu as pltpu
from jax.sharding import PartitionSpec as P

SEQ = 64
CHAN = 4
BLOCK = 512
LANES = 128
ROWS = 256
FILTERS = SEQ // CHAN
FULL = 2 * ROWS * LANES
VMEM_LIMIT = 60 * 1024 * 1024

BF16 = jnp.bfloat16
F32 = jnp.float32
MESH = pl.DeviceIdType.MESH


def split_table(table):
    high = table.astype(ml_dtypes.bfloat16)
    low = (table - high.astype(np.float64)).astype(ml_dtypes.bfloat16)
    return high, low


@functools.lru_cache(maxsize=None)
def tables():
    k1 = np.arange(ROWS)
    a = np.arange(ROWS)
    b = np.arange(LANES)
    outer = 2 * np.pi * ((a[None, :] * (2 * k1[:, None] + 1)) % 1024) / 1024.0
    first = np.concatenate([np.cos(outer), -np.sin(outer)], axis=0)
    last = first.T * (2.0 / FULL)
    twist = 2 * np.pi * (b[None, :] * (2 * k1[:, None] + 1)) / (2.0 * FULL)
    inner = 2 * np.pi * ((b[None, :] * b[:, None]) % LANES) / LANES
    cosine, sine = np.cos(inner), np.sin(inner)
    mid = np.block([[cosine, -sine], [sine, cosine]])
    back = np.block([[cosine, sine], [-sine, cosine]])
    first_h, first_l = split_table(first)
    last_h, last_l = split_table(last)
    mid_h, mid_l = split_table(mid)
    back_h, back_l = split_table(back)
    return (
        np.stack([first_h, first_l]),
        np.stack([last_h, last_l]),
        np.stack([mid_h, mid_l]),
        np.stack([back_h, back_l]),
        np.stack([np.cos(twist), np.sin(twist)]).astype(np.float32),
    )


def split(value):
    high = value.astype(BF16)
    low = (value - high.astype(F32)).astype(BF16)
    return high, low


def dot(left, right):
    return jnp.dot(left, right, preferred_element_type=F32)


def table_left(table, high, low):
    table_h, table_l = table[0], table[1]
    left = jnp.concatenate([table_h, table_h, table_l], axis=1)
    return dot(left, jnp.concatenate([high, low, high], axis=0))


def table_right(high, low, table):
    table_h, table_l = table[0], table[1]
    right = jnp.concatenate([table_h, table_h, table_l], axis=0)
    return dot(jnp.concatenate([high, low, high], axis=1), right)


def swap_matrix():
    row = lax.broadcasted_iota(jnp.int32, (256, 256), 0)
    col = lax.broadcasted_iota(jnp.int32, (256, 256), 1)
    hit = (row % 16 == col // 16) & (row // 16 == col % 16)
    return jnp.where(hit, 1.0, 0.0).astype(BF16)


def sort_matrix(outer, kinds, to_kinds):
    size = outer * kinds * 4
    row = lax.broadcasted_iota(jnp.int32, (size, size), 0)
    col = lax.broadcasted_iota(jnp.int32, (size, size), 1)
    by_kind, by_shard = (row, col) if to_kinds else (col, row)
    kind = by_kind // (outer * 4)
    shard = (by_kind // 4) % outer
    hit = by_shard == shard * (kinds * 4) + kind * 4 + by_kind % 4
    return jnp.where(hit, 1.0, 0.0).astype(BF16)


def delayed(value, steps):
    lane = lax.broadcasted_iota(jnp.int32, (ROWS, LANES), 1)
    row = lax.broadcasted_iota(jnp.int32, (ROWS, LANES), 0)
    turned = pltpu.roll(value, steps, 1)
    above = jnp.where(row == 0, 0.0, pltpu.roll(turned, 1, 0))
    return jnp.where(lane < steps, above, turned)


def advanced(value, steps):
    lane = lax.broadcasted_iota(jnp.int32, (ROWS, LANES), 1)
    row = lax.broadcasted_iota(jnp.int32, (ROWS, LANES), 0)
    turned = pltpu.roll(value, LANES - steps, 1)
    below = jnp.where(row == ROWS - 1, 0.0, pltpu.roll(turned, ROWS - 1, 0))
    return jnp.where(lane >= LANES - steps, below, turned)


def kernel(
    q_hbm, k_hbm, v_hbm, g_hbm, filt_hbm, qt_hbm, kt_hbm, vt_hbm, gain_hbm,
    first_hbm, last_hbm, mid_hbm, back_hbm, twist_hbm,
    out_hbm,
    q_ref, k_ref, v_ref, g_ref, filt_ref, qt_ref, kt_ref, vt_ref, gain_ref,
    first_ref, last_ref, mid_ref, back_ref, twist_ref,
    send_x, recv_x, send_f, recv_f, send_y, recv_y,
    input_sem, taps_sem, table_sem, out_sem, send_x_sem, recv_x_sem, send_f_sem, recv_f_sem,
    share_send_sem, share_recv_sem, send_y_sem, recv_y_sem,
):
    me = lax.axis_index("seq")
    group = lax.axis_index("chan")
    me_z, me_x, me_y = me // 8, (me // 2) % 4, me % 2

    def partner(step):
        dz = (step * 3) % 8
        dx = (step // 8) % 4
        dy = step // 32
        return ((me_z + dz) % 8) * 8 + ((me_x + dx) % 4) * 2 + (me_y + dy) % 2

    def copies(pairs, sems):
        return [
            pltpu.make_async_copy(source, target, sems.at[index])
            for index, (source, target) in enumerate(pairs)
        ]

    input_copies = copies(
        [(filt_hbm, filt_ref), (q_hbm, q_ref), (k_hbm, k_ref), (v_hbm, v_ref), (g_hbm, g_ref)],
        input_sem,
    )
    taps_copies = copies(
        [(qt_hbm, qt_ref), (kt_hbm, kt_ref), (vt_hbm, vt_ref), (gain_hbm, gain_ref)], taps_sem
    )
    table_copies = copies(
        [
            (first_hbm, first_ref),
            (mid_hbm, mid_ref),
            (twist_hbm, twist_ref),
            (back_hbm, back_ref),
            (last_hbm, last_ref),
        ],
        table_sem,
    )
    for copy in input_copies:
        copy.start()

    barrier = pltpu.get_barrier_semaphore()

    def greet(step, carry):
        pl.semaphore_signal(barrier, inc=1, device_id={"seq": partner(step)}, device_id_type=MESH)
        return carry

    lax.fori_loop(1, SEQ, greet, 0)
    source_group = me // FILTERS

    def greet_source(step, carry):
        source = group * FILTERS + (me + step) % FILTERS

        @pl.when(jnp.logical_not((source == me) & (source_group == group)))
        def _():
            pl.semaphore_signal(
                barrier, inc=1, device_id={"seq": source, "chan": source_group}, device_id_type=MESH
            )

        return carry

    lax.fori_loop(0, FILTERS, greet_source, 0)
    for step in range(1, CHAN):
        pl.semaphore_signal(
            barrier, inc=1, device_id={"chan": (group + step) % CHAN}, device_id_type=MESH
        )
    for copy in taps_copies + table_copies:
        copy.start()
    for copy in input_copies:
        copy.wait()

    filt_h, filt_l = split(filt_ref[...])
    pieces = [part[:, LANES * j : LANES * (j + 1)] for part in (filt_h, filt_l) for j in range(4)]
    row = lax.broadcasted_iota(jnp.int32, (128, 128), 0)
    col = lax.broadcasted_iota(jnp.int32, (128, 128), 1)
    regroup = jnp.where((row % 8 == col // 16) & (row // 8 == col % 16), 1.0, 0.0).astype(BF16)
    send_f[...] = dot(regroup, jnp.concatenate(pieces, axis=0)).astype(BF16).reshape(FILTERS, 8, LANES)
    swap = swap_matrix()
    for m in range(4):
        pieces = [
            ref[16 * m : 16 * (m + 1), LANES * j : LANES * (j + 1)]
            for ref in (q_ref, k_ref, v_ref, g_ref)
            for j in range(4)
        ]
        mixed_rows = dot(swap, jnp.concatenate(pieces, axis=0)).astype(BF16)
        send_x[16 * m : 16 * (m + 1)] = mixed_rows.reshape(16, 16, LANES)

    own_filter = (me // FILTERS == group) & (source_group == group)
    pl.semaphore_wait(barrier, SEQ - 1 + FILTERS + CHAN - 1 - own_filter.astype(jnp.int32))

    def send_filter(step, carry):
        r = (me + step) % FILTERS
        target = group * FILTERS + r
        to_self = (target == me) & (source_group == group)

        @pl.when(to_self)
        def _():
            pltpu.make_async_copy(send_f.at[r], recv_f.at[me], recv_f_sem).start()

        @pl.when(jnp.logical_not(to_self))
        def _():
            pltpu.make_async_remote_copy(
                src_ref=send_f.at[r],
                dst_ref=recv_f.at[me],
                send_sem=send_f_sem,
                recv_sem=recv_f_sem,
                device_id={"seq": target, "chan": source_group},
                device_id_type=MESH,
            ).start()

        return carry

    lax.fori_loop(0, FILTERS, send_filter, 0)

    pltpu.make_async_copy(send_x.at[me], recv_x.at[me], recv_x_sem).start()

    def send_inputs(step, carry):
        target = partner(step)
        pltpu.make_async_remote_copy(
            src_ref=send_x.at[target],
            dst_ref=recv_x.at[me],
            send_sem=send_x_sem,
            recv_sem=recv_x_sem,
            device_id={"seq": target},
            device_id_type=MESH,
        ).start()
        return carry

    lax.fori_loop(1, SEQ, send_inputs, 0)

    part = recv_f.at[pl.ds(group * FILTERS, FILTERS)]
    pltpu.make_async_copy(part, part, recv_f_sem).wait()
    for step in range(1, CHAN):
        pltpu.make_async_remote_copy(
            src_ref=part,
            dst_ref=part,
            send_sem=share_send_sem,
            recv_sem=share_recv_sem,
            device_id={"chan": (group + step) % CHAN},
            device_id_type=MESH,
        ).start()
    three = recv_f.at[pl.ds(0, (CHAN - 1) * FILTERS)]
    pltpu.make_async_copy(three, three, share_recv_sem).wait()

    sort_f = sort_matrix(32, 2, True)
    filt_hi, filt_lo = [], []
    for m in range(2):
        got = recv_f[32 * m : 32 * (m + 1)].reshape(256, LANES)
        rows = dot(sort_f, got).astype(BF16)
        filt_hi.append(rows[:128])
        filt_lo.append(rows[128:])

    for copy in taps_copies + table_copies:
        copy.wait()

    pltpu.make_async_copy(recv_x, recv_x, recv_x_sem).wait()
    sort_x = sort_matrix(16, 4, True)
    parts = []
    for m in range(4):
        got = recv_x[16 * m : 16 * (m + 1)].reshape(256, LANES)
        parts.append(dot(sort_x, got))
    query, key, value, cotangent = (
        jnp.concatenate([rows[64 * i : 64 * (i + 1)] for rows in parts], axis=0) for i in range(4)
    )

    def causal_taps(signal, taps):
        return (
            taps[0, me] * signal + taps[1, me] * delayed(signal, 1) + taps[2, me] * delayed(signal, 2)
        )

    def reverse_taps(signal, taps):
        return (
            taps[0, me] * signal + taps[1, me] * advanced(signal, 1) + taps[2, me] * advanced(signal, 2)
        )

    short_q = causal_taps(query, qt_ref)
    short_k = causal_taps(key, kt_ref)
    short_v = causal_taps(value, vt_ref)
    product = short_k * short_v
    grad_mixed = cotangent * short_q

    prod_h, prod_l = split(product)
    grad_h, grad_l = split(grad_mixed)
    high = jnp.concatenate([jnp.concatenate(filt_hi, axis=0), prod_h, grad_h], axis=1)
    low = jnp.concatenate([jnp.concatenate(filt_lo, axis=0), prod_l, grad_l], axis=1)
    outer = table_left(first_ref, high, low)
    cosine, sine = twist_ref[0], twist_ref[1]

    def spectrum(index):
        real = outer[:ROWS, LANES * index : LANES * (index + 1)]
        imag = outer[ROWS:, LANES * index : LANES * (index + 1)]
        turned = jnp.concatenate([real * cosine + imag * sine, imag * cosine - real * sine], axis=1)
        whole = table_right(*split(turned), mid_ref)
        return whole[:, :LANES], whole[:, LANES:]

    filt_re, filt_im = spectrum(0)

    def inverse(real, imag):
        back = table_right(*split(jnp.concatenate([real, imag], axis=1)), back_ref)
        real, imag = back[:, :LANES], back[:, LANES:]
        return jnp.concatenate([real * cosine - imag * sine, imag * cosine + real * sine], axis=0)

    prod_re, prod_im = spectrum(1)
    fwd = inverse(filt_re * prod_re - filt_im * prod_im, filt_re * prod_im + filt_im * prod_re)
    grad_re, grad_im = spectrum(2)
    bwd = inverse(filt_re * grad_re + filt_im * grad_im, filt_re * grad_im - filt_im * grad_re)
    both = table_left(last_ref, *split(jnp.concatenate([fwd, bwd], axis=1)))
    causal, backward = both[:, :LANES], both[:, LANES:]

    gain = gain_ref[me]
    mixed = causal + gain * product
    gated = short_q * mixed
    grad_product = backward + gain * grad_mixed
    outs = [
        gated.astype(BF16),
        reverse_taps(cotangent * mixed, qt_ref).astype(BF16),
        reverse_taps(grad_product * short_v, kt_ref).astype(BF16),
        reverse_taps(grad_product * short_k, vt_ref).astype(BF16),
    ]
    sort_y = sort_matrix(16, 4, False)
    for m in range(4):
        rows = jnp.concatenate([out[64 * m : 64 * (m + 1)] for out in outs], axis=0)
        send_y[16 * m : 16 * (m + 1)] = dot(sort_y, rows).astype(BF16).reshape(16, 16, LANES)

    pltpu.make_async_copy(send_y.at[me], recv_y.at[me], recv_y_sem).start()

    def send_outputs(step, carry):
        target = partner(step)
        pltpu.make_async_remote_copy(
            src_ref=send_y.at[target],
            dst_ref=recv_y.at[me],
            send_sem=send_y_sem,
            recv_sem=recv_y_sem,
            device_id={"seq": target},
            device_id_type=MESH,
        ).start()
        return carry

    lax.fori_loop(1, SEQ, send_outputs, 0)

    sent = send_x.at[pl.ds(0, SEQ - 1)]
    pltpu.make_async_copy(sent, sent, send_x_sem).wait()
    pltpu.make_async_copy(three, three, share_send_sem).wait()

    @pl.when(own_filter)
    def _():
        some = send_f.at[pl.ds(0, FILTERS - 1)]
        pltpu.make_async_copy(some, some, send_f_sem).wait()

    @pl.when(jnp.logical_not(own_filter))
    def _():
        pltpu.make_async_copy(send_f, send_f, send_f_sem).wait()

    pltpu.make_async_copy(recv_y, recv_y, recv_y_sem).wait()
    result = pltpu.make_async_copy(recv_y, out_hbm, out_sem)
    result.start()
    sent = send_y.at[pl.ds(0, SEQ - 1)]
    pltpu.make_async_copy(sent, sent, send_y_sem).wait()
    result.wait()


def scatter_kernel(in_hbm, *refs):
    out_hbm, (in_ref, *out_refs), (in_sem, out_sem) = refs[:4], refs[4:9], refs[9:]
    copy = pltpu.make_async_copy(in_hbm, in_ref, in_sem)
    copy.start()
    swap = swap_matrix()
    copy.wait()
    for m in range(4):
        rows = dot(swap, in_ref[16 * m : 16 * (m + 1)].reshape(256, LANES)).astype(BF16)
        for i, ref in enumerate(out_refs):
            for j in range(4):
                at = (4 * i + j) * 16
                ref[16 * m : 16 * (m + 1), LANES * j : LANES * (j + 1)] = rows[at : at + 16]
    stores = [
        pltpu.make_async_copy(ref, hbm, out_sem.at[i])
        for i, (ref, hbm) in enumerate(zip(out_refs, out_hbm))
    ]
    for store in stores:
        store.start()
    for store in stores:
        store.wait()


def body(q, k, v, long_filter, q_taps, k_taps, v_taps, gain, cotangent):
    constants = [jnp.asarray(table) for table in tables()]
    anywhere = pl.BlockSpec(memory_space=pl.ANY)
    block = pltpu.VMEM((SEQ, BLOCK), BF16)
    exchange = pltpu.VMEM((SEQ, 16, LANES), BF16)
    arrived = pl.pallas_call(
        kernel,
        out_shape=jax.ShapeDtypeStruct((SEQ, 16, LANES), BF16),
        in_specs=[anywhere] * 14,
        out_specs=anywhere,
        scratch_shapes=[block] * 4
        + [pltpu.VMEM((FILTERS, BLOCK), F32)]
        + [pltpu.SMEM((3, SEQ), F32)] * 3
        + [pltpu.SMEM((SEQ,), F32)]
        + [
            pltpu.VMEM((2, 512, 256), BF16),
            pltpu.VMEM((2, 256, 512), BF16),
            pltpu.VMEM((2, 256, 256), BF16),
            pltpu.VMEM((2, 256, 256), BF16),
            pltpu.VMEM((2, ROWS, LANES), F32),
            exchange,
            exchange,
            pltpu.VMEM((FILTERS, 8, LANES), BF16),
            pltpu.VMEM((SEQ, 8, LANES), BF16),
            exchange,
            exchange,
            pltpu.SemaphoreType.DMA((5,)),
            pltpu.SemaphoreType.DMA((4,)),
            pltpu.SemaphoreType.DMA((5,)),
        ]
        + [pltpu.SemaphoreType.DMA] * 9,
        compiler_params=pltpu.CompilerParams(
            collective_id=0, has_side_effects=True, vmem_limit_bytes=VMEM_LIMIT
        ),
        name="hyena",
    )(q, k, v, cotangent, long_filter, q_taps, k_taps, v_taps, gain, *constants)
    return pl.pallas_call(
        scatter_kernel,
        out_shape=[jax.ShapeDtypeStruct((SEQ, BLOCK), BF16)] * 4,
        in_specs=[anywhere],
        out_specs=[anywhere] * 4,
        scratch_shapes=[exchange] + [block] * 4 + [pltpu.SemaphoreType.DMA, pltpu.SemaphoreType.DMA((4,))],
        compiler_params=pltpu.CompilerParams(vmem_limit_bytes=VMEM_LIMIT),
        name="scatter_rows",
    )(arrived)


def solution(mesh):
    in_specs = (
        P("chan", "seq"),
        P("chan", "seq"),
        P("chan", "seq"),
        P("chan", "seq"),
        P(None, "chan"),
        P(None, "chan"),
        P(None, "chan"),
        P("chan"),
        P("chan", "seq"),
    )
    out_specs = (P("chan", "seq"),) * 4
    return jax.shard_map(body, mesh=mesh, in_specs=in_specs, out_specs=out_specs, check_vma=False)
```

```python
import functools

import jax
import jax.numpy as jnp
import ml_dtypes
import numpy as np
from jax import lax
from jax.experimental import pallas as pl
from jax.experimental.pallas import tpu as pltpu
from jax.sharding import PartitionSpec as P

SEQ = 64
CHAN = 4
BLOCK = 512
LANES = 128
ROWS = 256
FILTERS = SEQ // CHAN
FULL = 2 * ROWS * LANES
VMEM_LIMIT = 60 * 1024 * 1024

BF16 = jnp.bfloat16
F32 = jnp.float32
MESH = pl.DeviceIdType.MESH


def split_table(table):
    high = table.astype(ml_dtypes.bfloat16)
    low = (table - high.astype(np.float64)).astype(ml_dtypes.bfloat16)
    return high, low


@functools.lru_cache(maxsize=None)
def tables():
    k1 = np.arange(ROWS)
    a = np.arange(ROWS)
    b = np.arange(LANES)
    outer = 2 * np.pi * ((a[None, :] * (2 * k1[:, None] + 1)) % 1024) / 1024.0
    first = np.concatenate([np.cos(outer), -np.sin(outer)], axis=0)
    last = first.T * (2.0 / FULL)
    twist = 2 * np.pi * (b[None, :] * (2 * k1[:, None] + 1)) / (2.0 * FULL)
    inner = 2 * np.pi * ((b[None, :] * b[:, None]) % LANES) / LANES
    cosine, sine = np.cos(inner), np.sin(inner)
    mid = np.block([[cosine, -sine], [sine, cosine]])
    back = np.block([[cosine, sine], [-sine, cosine]])
    first_h, first_l = split_table(first)
    last_h, last_l = split_table(last)
    mid_h, mid_l = split_table(mid)
    back_h, back_l = split_table(back)
    return (
        np.stack([first_h, first_l]),
        np.stack([last_h, last_l]),
        np.stack([mid_h, mid_l]),
        np.stack([back_h, back_l]),
        np.stack([np.cos(twist), np.sin(twist)]).astype(np.float32),
    )


def split(value):
    high = value.astype(BF16)
    low = (value - high.astype(F32)).astype(BF16)
    return high, low


def dot(left, right):
    return jnp.dot(left, right, preferred_element_type=F32)


def table_left(table, high, low):
    table_h, table_l = table[0], table[1]
    left = jnp.concatenate([table_h, table_h, table_l], axis=1)
    return dot(left, jnp.concatenate([high, low, high], axis=0))


def table_right(high, low, table):
    table_h, table_l = table[0], table[1]
    right = jnp.concatenate([table_h, table_h, table_l], axis=0)
    return dot(jnp.concatenate([high, low, high], axis=1), right)


def swap_matrix():
    row = lax.broadcasted_iota(jnp.int32, (256, 256), 0)
    col = lax.broadcasted_iota(jnp.int32, (256, 256), 1)
    hit = (row % 16 == col // 16) & (row // 16 == col % 16)
    return jnp.where(hit, 1.0, 0.0).astype(BF16)


def sort_matrix(outer, kinds, to_kinds):
    size = outer * kinds * 4
    row = lax.broadcasted_iota(jnp.int32, (size, size), 0)
    col = lax.broadcasted_iota(jnp.int32, (size, size), 1)
    by_kind, by_shard = (row, col) if to_kinds else (col, row)
    kind = by_kind // (outer * 4)
    shard = (by_kind // 4) % outer
    hit = by_shard == shard * (kinds * 4) + kind * 4 + by_kind % 4
    return jnp.where(hit, 1.0, 0.0).astype(BF16)


def delayed(value, steps):
    lane = lax.broadcasted_iota(jnp.int32, (ROWS, LANES), 1)
    row = lax.broadcasted_iota(jnp.int32, (ROWS, LANES), 0)
    turned = pltpu.roll(value, steps, 1)
    above = jnp.where(row == 0, 0.0, pltpu.roll(turned, 1, 0))
    return jnp.where(lane < steps, above, turned)


def advanced(value, steps):
    lane = lax.broadcasted_iota(jnp.int32, (ROWS, LANES), 1)
    row = lax.broadcasted_iota(jnp.int32, (ROWS, LANES), 0)
    turned = pltpu.roll(value, LANES - steps, 1)
    below = jnp.where(row == ROWS - 1, 0.0, pltpu.roll(turned, ROWS - 1, 0))
    return jnp.where(lane >= LANES - steps, below, turned)


def kernel(
    q_hbm, k_hbm, v_hbm, g_hbm, filt_hbm, qt_hbm, kt_hbm, vt_hbm, gain_hbm,
    first_hbm, last_hbm, mid_hbm, back_hbm, twist_hbm,
    recv_y,
    q_ref, k_ref, v_ref, g_ref, filt_ref, qt_ref, kt_ref, vt_ref, gain_ref,
    first_ref, last_ref, mid_ref, back_ref, twist_ref,
    send_x, recv_x, send_f, recv_f, send_y, filt_spec,
    input_sem, taps_sem, table_sem, send_x_sem, recv_x_sem, send_f_sem, recv_f_sem,
    share_send_sem, share_recv_sem, far_sem, send_y_sem, recv_y_sem,
):
    me = lax.axis_index("seq")
    group = lax.axis_index("chan")
    home, part_of = me % CHAN, me // FILTERS
    channel = home * FILTERS + me // CHAN
    core_peer, far_peer = group + 1 - 2 * (group % 2), (group + 2) % CHAN
    planes = [(me // 8 + dz) % 8 * 8 for dz in (0, 4, 1, 7, 3, 5, 2, 6)]
    highs = [(me // 4 + dx) % 2 * 4 for dx in range(2)]
    lows = [home, home + 1 - 2 * (me % 2), (home + 2) % 4, (home + 2) % 4 + 1 - 2 * (me % 2)]

    def copies(pairs, sems):
        return [
            pltpu.make_async_copy(source, target, sems.at[index])
            for index, (source, target) in enumerate(pairs)
        ]

    input_copies = copies(
        [(filt_hbm, filt_ref), (q_hbm, q_ref), (k_hbm, k_ref), (v_hbm, v_ref), (g_hbm, g_ref)],
        input_sem,
    )
    taps_copies = copies(
        [(qt_hbm, qt_ref), (kt_hbm, kt_ref), (vt_hbm, vt_ref), (gain_hbm, gain_ref)], taps_sem
    )
    table_copies = copies(
        [
            (first_hbm, first_ref),
            (mid_hbm, mid_ref),
            (twist_hbm, twist_ref),
            (back_hbm, back_ref),
            (last_hbm, last_ref),
        ],
        table_sem,
    )
    for copy in input_copies:
        copy.start()

    barrier = pltpu.get_barrier_semaphore()

    for low in lows:
        for high in highs:
            for plane in planes:
                if low is lows[0] and high is highs[0] and plane is planes[0]:
                    continue
                pl.semaphore_signal(
                    barrier, inc=1, device_id={"seq": plane + high + low}, device_id_type=MESH
                )
    own_filter = (home == group) & (part_of == group)

    def greet_source(step, carry):
        source = group * FILTERS + (me + step) % FILTERS

        @pl.when(jnp.logical_not((source == me) & (home == group)))
        def _():
            pl.semaphore_signal(
                barrier, inc=1, device_id={"seq": source, "chan": home}, device_id_type=MESH
            )

        return carry

    lax.fori_loop(0, FILTERS, greet_source, 0)
    for peer in (core_peer, far_peer):
        pl.semaphore_signal(barrier, inc=1, device_id={"chan": peer}, device_id_type=MESH)
    for copy in taps_copies + table_copies:
        copy.start()
    input_copies[0].wait()

    filt_h, filt_l = split(filt_ref[...])
    pieces = [part[:, LANES * j : LANES * (j + 1)] for part in (filt_h, filt_l) for j in range(4)]
    row = lax.broadcasted_iota(jnp.int32, (128, 128), 0)
    col = lax.broadcasted_iota(jnp.int32, (128, 128), 1)
    regroup = jnp.where((row % 8 == col // 16) & (row // 8 == col % 16), 1.0, 0.0).astype(BF16)
    send_f[...] = dot(regroup, jnp.concatenate(pieces, axis=0)).astype(BF16).reshape(FILTERS, 8, LANES)
    swap = swap_matrix()
    for copy in input_copies[1:]:
        copy.wait()

    def regroup_inputs(low):
        pieces = [
            ref[pl.ds(pl.multiple_of(16 * low, 16), 16), LANES * j : LANES * (j + 1)]
            for ref in (q_ref, k_ref, v_ref, g_ref)
            for j in range(4)
        ]
        rows = dot(swap, jnp.concatenate(pieces, axis=0)).astype(BF16)
        send_x[pl.ds(16 * low, 16)] = rows.reshape(16, 16, LANES)

    regroup_inputs(lows[0])
    pl.semaphore_wait(barrier, SEQ - 1 + FILTERS + 2 - own_filter.astype(jnp.int32))

    def send_filter(step, carry):
        r = (me + step) % FILTERS
        target = CHAN * r + group
        to_self = (target == me) & (part_of == group)

        @pl.when(to_self)
        def _():
            pltpu.make_async_copy(send_f.at[r], recv_f.at[me], recv_f_sem).start()

        @pl.when(jnp.logical_not(to_self))
        def _():
            pltpu.make_async_remote_copy(
                src_ref=send_f.at[r],
                dst_ref=recv_f.at[me],
                send_sem=send_f_sem,
                recv_sem=recv_f_sem,
                device_id={"seq": target, "chan": part_of},
                device_id_type=MESH,
            ).start()

        return carry

    lax.fori_loop(0, FILTERS, send_filter, 0)

    pltpu.make_async_copy(send_x.at[channel], recv_x.at[me], recv_x_sem).start()
    for low in lows:
        if low is not lows[0]:
            regroup_inputs(low)
        for high in highs:
            for plane in planes:
                if low is lows[0] and high is highs[0] and plane is planes[0]:
                    continue
                pltpu.make_async_remote_copy(
                    src_ref=send_x.at[low * FILTERS + (plane + high) // CHAN],
                    dst_ref=recv_x.at[me],
                    send_sem=send_x_sem,
                    recv_sem=recv_x_sem,
                    device_id={"seq": plane + high + low},
                    device_id_type=MESH,
                ).start()

    def filter_part(index):
        return recv_f.at[pl.ds(index * FILTERS, FILTERS)]

    def share(index, peer, sem):
        pltpu.make_async_remote_copy(
            src_ref=filter_part(index),
            dst_ref=filter_part(index),
            send_sem=share_send_sem,
            recv_sem=sem,
            device_id={"chan": peer},
            device_id_type=MESH,
        ).start()

    pltpu.make_async_copy(filter_part(group), filter_part(group), recv_f_sem).wait()
    share(group, far_peer, far_sem)
    share(group, core_peer, share_recv_sem)
    pltpu.make_async_copy(filter_part(far_peer), filter_part(far_peer), far_sem).wait()
    share(far_peer, core_peer, share_recv_sem)
    two = recv_f.at[pl.ds(0, 2 * FILTERS)]
    pltpu.make_async_copy(two, two, share_recv_sem).wait()
    three = recv_f.at[pl.ds(0, (CHAN - 1) * FILTERS)]

    for copy in taps_copies + table_copies:
        copy.wait()

    cosine, sine = twist_ref[0], twist_ref[1]

    def spectrum(outer):
        real, imag = outer[:ROWS], outer[ROWS:]
        turned = jnp.concatenate([real * cosine + imag * sine, imag * cosine - real * sine], axis=1)
        whole = table_right(*split(turned), mid_ref)
        return whole[:, :LANES], whole[:, LANES:]

    sort_f = sort_matrix(32, 2, True)
    filt_hi, filt_lo = [], []
    for m in range(2):
        got = recv_f[32 * m : 32 * (m + 1)].reshape(256, LANES)
        rows = dot(sort_f, got).astype(BF16)
        filt_hi.append(rows[:128])
        filt_lo.append(rows[128:])
    filt_re, filt_im = spectrum(
        table_left(first_ref, jnp.concatenate(filt_hi, axis=0), jnp.concatenate(filt_lo, axis=0))
    )
    filt_spec[0] = filt_re
    filt_spec[1] = filt_im

    pltpu.make_async_copy(recv_x, recv_x, recv_x_sem).wait()
    sort_x = sort_matrix(16, 4, True)
    parts = []
    for m in range(4):
        got = recv_x[16 * m : 16 * (m + 1)].reshape(256, LANES)
        parts.append(dot(sort_x, got))
    query, key, value, cotangent = (
        jnp.concatenate([rows[64 * i : 64 * (i + 1)] for rows in parts], axis=0) for i in range(4)
    )

    def causal_taps(signal, taps):
        return (
            taps[0, channel] * signal + taps[1, channel] * delayed(signal, 1) + taps[2, channel] * delayed(signal, 2)
        )

    def reverse_taps(signal, taps):
        return (
            taps[0, channel] * signal + taps[1, channel] * advanced(signal, 1) + taps[2, channel] * advanced(signal, 2)
        )

    short_q = causal_taps(query, qt_ref)
    short_k = causal_taps(key, kt_ref)
    short_v = causal_taps(value, vt_ref)
    product = short_k * short_v
    grad_mixed = cotangent * short_q

    outer = table_left(first_ref, *split(jnp.concatenate([product, grad_mixed], axis=1)))
    filt_re, filt_im = filt_spec[0], filt_spec[1]

    def inverse(real, imag):
        back = table_right(*split(jnp.concatenate([real, imag], axis=1)), back_ref)
        real, imag = back[:, :LANES], back[:, LANES:]
        return jnp.concatenate([real * cosine - imag * sine, imag * cosine + real * sine], axis=0)

    prod_re, prod_im = spectrum(outer[:, :LANES])
    fwd = inverse(filt_re * prod_re - filt_im * prod_im, filt_re * prod_im + filt_im * prod_re)
    grad_re, grad_im = spectrum(outer[:, LANES:])
    bwd = inverse(filt_re * grad_re + filt_im * grad_im, filt_re * grad_im - filt_im * grad_re)
    both = table_left(last_ref, *split(jnp.concatenate([fwd, bwd], axis=1)))
    causal, backward = both[:, :LANES], both[:, LANES:]

    gain = gain_ref[channel]
    mixed = causal + gain * product
    gated = short_q * mixed
    grad_product = backward + gain * grad_mixed
    outs = [
        gated.astype(BF16),
        reverse_taps(cotangent * mixed, qt_ref).astype(BF16),
        reverse_taps(grad_product * short_v, kt_ref).astype(BF16),
        reverse_taps(grad_product * short_k, vt_ref).astype(BF16),
    ]
    sort_y = sort_matrix(16, 4, False)
    for m in range(4):
        rows = jnp.concatenate([out[64 * m : 64 * (m + 1)] for out in outs], axis=0)
        send_y[16 * m : 16 * (m + 1)] = dot(sort_y, rows).astype(BF16).reshape(16, 16, LANES)

    pltpu.make_async_copy(send_y.at[me], recv_y.at[channel], recv_y_sem).start()
    for low in lows:
        for high in highs:
            for plane in planes:
                if low is lows[0] and high is highs[0] and plane is planes[0]:
                    continue
                pltpu.make_async_remote_copy(
                    src_ref=send_y.at[plane + high + low],
                    dst_ref=recv_y.at[channel],
                    send_sem=send_y_sem,
                    recv_sem=recv_y_sem,
                    device_id={"seq": plane + high + low},
                    device_id_type=MESH,
                ).start()

    sent = send_x.at[pl.ds(0, SEQ - 1)]
    pltpu.make_async_copy(sent, sent, send_x_sem).wait()
    pltpu.make_async_copy(three, three, share_send_sem).wait()

    @pl.when(own_filter)
    def _():
        some = send_f.at[pl.ds(0, FILTERS - 1)]
        pltpu.make_async_copy(some, some, send_f_sem).wait()

    @pl.when(jnp.logical_not(own_filter))
    def _():
        pltpu.make_async_copy(send_f, send_f, send_f_sem).wait()

    pltpu.make_async_copy(recv_y, recv_y, recv_y_sem).wait()
    sent = send_y.at[pl.ds(0, SEQ - 1)]
    pltpu.make_async_copy(sent, sent, send_y_sem).wait()


def scatter_kernel(in_ref, *refs):
    out_hbm, out_refs, out_sem = refs[:4], refs[4:8], refs[8]
    swap = swap_matrix()
    for m in range(4):
        rows = dot(swap, in_ref[16 * m : 16 * (m + 1)].reshape(256, LANES)).astype(BF16)
        for i, ref in enumerate(out_refs):
            for j in range(4):
                at = (4 * i + j) * 16
                ref[16 * m : 16 * (m + 1), LANES * j : LANES * (j + 1)] = rows[at : at + 16]
    stores = [
        pltpu.make_async_copy(ref, hbm, out_sem.at[i])
        for i, (ref, hbm) in enumerate(zip(out_refs, out_hbm))
    ]
    for store in stores:
        store.start()
    for store in stores:
        store.wait()


def body(q, k, v, long_filter, q_taps, k_taps, v_taps, gain, cotangent):
    constants = [jnp.asarray(table) for table in tables()]
    vmem = pl.BlockSpec(memory_space=pltpu.VMEM)
    anywhere = pl.BlockSpec(memory_space=pl.ANY)
    block = pltpu.VMEM((SEQ, BLOCK), BF16)
    exchange = pltpu.VMEM((SEQ, 16, LANES), BF16)
    arrived = pl.pallas_call(
        kernel,
        out_shape=jax.ShapeDtypeStruct((SEQ, 16, LANES), BF16),
        in_specs=[anywhere] * 14,
        out_specs=vmem,
        scratch_shapes=[block] * 4
        + [pltpu.VMEM((FILTERS, BLOCK), F32)]
        + [pltpu.SMEM((3, SEQ), F32)] * 3
        + [pltpu.SMEM((SEQ,), F32)]
        + [
            pltpu.VMEM((2, 512, 256), BF16),
            pltpu.VMEM((2, 256, 512), BF16),
            pltpu.VMEM((2, 256, 256), BF16),
            pltpu.VMEM((2, 256, 256), BF16),
            pltpu.VMEM((2, ROWS, LANES), F32),
            exchange,
            exchange,
            pltpu.VMEM((FILTERS, 8, LANES), BF16),
            pltpu.VMEM((SEQ, 8, LANES), BF16),
            exchange,
            pltpu.VMEM((2, ROWS, LANES), F32),
            pltpu.SemaphoreType.DMA((5,)),
            pltpu.SemaphoreType.DMA((4,)),
            pltpu.SemaphoreType.DMA((5,)),
        ]
        + [pltpu.SemaphoreType.DMA] * 9,
        compiler_params=pltpu.CompilerParams(
            collective_id=0, has_side_effects=True, vmem_limit_bytes=VMEM_LIMIT
        ),
        name="hyena",
    )(q, k, v, cotangent, long_filter, q_taps, k_taps, v_taps, gain, *constants)
    return pl.pallas_call(
        scatter_kernel,
        out_shape=[jax.ShapeDtypeStruct((SEQ, BLOCK), BF16)] * 4,
        in_specs=[vmem],
        out_specs=[anywhere] * 4,
        scratch_shapes=[block] * 4 + [pltpu.SemaphoreType.DMA((4,))],
        compiler_params=pltpu.CompilerParams(vmem_limit_bytes=VMEM_LIMIT),
        name="scatter_rows",
    )(arrived)


def solution(mesh):
    in_specs = (
        P("chan", "seq"),
        P("chan", "seq"),
        P("chan", "seq"),
        P("chan", "seq"),
        P(None, "chan"),
        P(None, "chan"),
        P(None, "chan"),
        P("chan"),
        P("chan", "seq"),
    )
    out_specs = (P("chan", "seq"),) * 4
    return jax.shard_map(body, mesh=mesh, in_specs=in_specs, out_specs=out_specs, check_vma=False)
```

```python
import functools

import jax
import jax.numpy as jnp
import ml_dtypes
import numpy as np
from jax import lax
from jax.experimental import pallas as pl
from jax.experimental.pallas import tpu as pltpu
from jax.sharding import PartitionSpec as P

SEQ = 64
CHAN = 4
BLOCK = 512
LANES = 128
ROWS = 256
FILTERS = SEQ // CHAN
FULL = 2 * ROWS * LANES
VMEM_LIMIT = 60 * 1024 * 1024

BF16 = jnp.bfloat16
F32 = jnp.float32
MESH = pl.DeviceIdType.MESH


def split_table(table):
    high = table.astype(ml_dtypes.bfloat16)
    low = (table - high.astype(np.float64)).astype(ml_dtypes.bfloat16)
    return high, low


@functools.lru_cache(maxsize=None)
def tables():
    k1 = np.arange(ROWS)
    a = np.arange(ROWS)
    b = np.arange(LANES)
    outer = 2 * np.pi * ((a[None, :] * (2 * k1[:, None] + 1)) % 1024) / 1024.0
    first = np.concatenate([np.cos(outer), -np.sin(outer)], axis=0)
    last = first.T * (2.0 / FULL)
    twist = 2 * np.pi * (b[None, :] * (2 * k1[:, None] + 1)) / (2.0 * FULL)
    inner = 2 * np.pi * ((b[None, :] * b[:, None]) % LANES) / LANES
    cosine, sine = np.cos(inner), np.sin(inner)
    mid = np.block([[cosine, -sine], [sine, cosine]])
    back = np.block([[cosine, sine], [-sine, cosine]])
    first_h, first_l = split_table(first)
    last_h, last_l = split_table(last)
    mid_h, mid_l = split_table(mid)
    back_h, back_l = split_table(back)
    return (
        np.stack([first_h, first_l]),
        np.stack([last_h, last_l]),
        np.stack([mid_h, mid_l]),
        np.stack([back_h, back_l]),
        np.stack([np.cos(twist), np.sin(twist)]).astype(np.float32),
    )


def split(value):
    high = value.astype(BF16)
    low = (value - high.astype(F32)).astype(BF16)
    return high, low


def dot(left, right):
    return jnp.dot(left, right, preferred_element_type=F32)


def table_left(table, high, low):
    table_h, table_l = table[0], table[1]
    left = jnp.concatenate([table_h, table_h, table_l], axis=1)
    return dot(left, jnp.concatenate([high, low, high], axis=0))


def table_right(high, low, table):
    table_h, table_l = table[0], table[1]
    right = jnp.concatenate([table_h, table_h, table_l], axis=0)
    return dot(jnp.concatenate([high, low, high], axis=1), right)


def swap_matrix():
    row = lax.broadcasted_iota(jnp.int32, (256, 256), 0)
    col = lax.broadcasted_iota(jnp.int32, (256, 256), 1)
    hit = (row % 16 == col // 16) & (row // 16 == col % 16)
    return jnp.where(hit, 1.0, 0.0).astype(BF16)


def sort_matrix(outer, kinds, to_kinds):
    size = outer * kinds * 4
    row = lax.broadcasted_iota(jnp.int32, (size, size), 0)
    col = lax.broadcasted_iota(jnp.int32, (size, size), 1)
    by_kind, by_shard = (row, col) if to_kinds else (col, row)
    kind = by_kind // (outer * 4)
    shard = (by_kind // 4) % outer
    hit = by_shard == shard * (kinds * 4) + kind * 4 + by_kind % 4
    return jnp.where(hit, 1.0, 0.0).astype(BF16)


def delayed(value, steps):
    lane = lax.broadcasted_iota(jnp.int32, (ROWS, LANES), 1)
    row = lax.broadcasted_iota(jnp.int32, (ROWS, LANES), 0)
    turned = pltpu.roll(value, steps, 1)
    above = jnp.where(row == 0, 0.0, pltpu.roll(turned, 1, 0))
    return jnp.where(lane < steps, above, turned)


def advanced(value, steps):
    lane = lax.broadcasted_iota(jnp.int32, (ROWS, LANES), 1)
    row = lax.broadcasted_iota(jnp.int32, (ROWS, LANES), 0)
    turned = pltpu.roll(value, LANES - steps, 1)
    below = jnp.where(row == ROWS - 1, 0.0, pltpu.roll(turned, ROWS - 1, 0))
    return jnp.where(lane >= LANES - steps, below, turned)


def kernel(
    q_hbm, k_hbm, v_hbm, g_hbm, filt_hbm, qt_hbm, kt_hbm, vt_hbm, gain_hbm,
    first_hbm, last_hbm, mid_hbm, back_hbm, twist_hbm,
    recv_y,
    q_ref, k_ref, v_ref, g_ref, filt_ref, qt_ref, kt_ref, vt_ref, gain_ref,
    first_ref, last_ref, mid_ref, back_ref, twist_ref,
    send_x, recv_x, send_f, recv_f, send_y, spec,
    input_sem, taps_sem, table_sem, send_x_sem, recv_x_sem, send_f_sem, recv_f_sem,
    share_send_sem, share_recv_sem, far_sem, send_y_sem, recv_y_sem,
):
    me = lax.axis_index("seq")
    group = lax.axis_index("chan")
    home, part_of = me % CHAN, me // FILTERS
    channel = home * FILTERS + me // CHAN
    core_peer, far_peer = group + 1 - 2 * (group % 2), (group + 2) % CHAN
    planes = [(me // 8 + dz) % 8 * 8 for dz in range(8)]
    highs = [(me // 4 + dx) % 2 * 4 for dx in range(2)]
    lows = [home, home + 1 - 2 * (me % 2), (home + 2) % 4, (home + 2) % 4 + 1 - 2 * (me % 2)]

    def hops(dz, high, low):
        return min(dz, 8 - dz) + (low // 2 if high == 0 else 2 - low // 2) + low % 2

    steps = [(dz, high, low) for low in range(4) for high in range(2) for dz in range(8)]
    steps = sorted(steps[1:], key=lambda step: -hops(*step))

    def copies(pairs, sems):
        return [
            pltpu.make_async_copy(source, target, sems.at[index])
            for index, (source, target) in enumerate(pairs)
        ]

    input_copies = copies(
        [(filt_hbm, filt_ref), (q_hbm, q_ref), (k_hbm, k_ref), (v_hbm, v_ref), (g_hbm, g_ref)],
        input_sem,
    )
    taps_copies = copies(
        [(qt_hbm, qt_ref), (kt_hbm, kt_ref), (vt_hbm, vt_ref), (gain_hbm, gain_ref)], taps_sem
    )
    table_copies = copies(
        [
            (first_hbm, first_ref),
            (mid_hbm, mid_ref),
            (twist_hbm, twist_ref),
            (back_hbm, back_ref),
            (last_hbm, last_ref),
        ],
        table_sem,
    )
    for copy in input_copies:
        copy.start()

    barrier = pltpu.get_barrier_semaphore()

    for dz, high, low in steps:
        partner = planes[dz] + highs[high] + lows[low]
        pl.semaphore_signal(barrier, inc=1, device_id={"seq": partner}, device_id_type=MESH)
    own_filter = (home == group) & (part_of == group)

    def greet_source(step, carry):
        source = group * FILTERS + (me + step) % FILTERS

        @pl.when(jnp.logical_not((source == me) & (home == group)))
        def _():
            pl.semaphore_signal(
                barrier, inc=1, device_id={"seq": source, "chan": home}, device_id_type=MESH
            )

        return carry

    lax.fori_loop(0, FILTERS, greet_source, 0)
    for peer in (core_peer, far_peer):
        pl.semaphore_signal(barrier, inc=1, device_id={"chan": peer}, device_id_type=MESH)
    for copy in taps_copies + table_copies:
        copy.start()
    input_copies[0].wait()

    filt_h, filt_l = split(filt_ref[...])
    pieces = [part[:, LANES * j : LANES * (j + 1)] for part in (filt_h, filt_l) for j in range(4)]
    row = lax.broadcasted_iota(jnp.int32, (128, 128), 0)
    col = lax.broadcasted_iota(jnp.int32, (128, 128), 1)
    regroup = jnp.where((row % 8 == col // 16) & (row // 8 == col % 16), 1.0, 0.0).astype(BF16)
    send_f[...] = dot(regroup, jnp.concatenate(pieces, axis=0)).astype(BF16).reshape(FILTERS, 8, LANES)
    swap = swap_matrix()
    for copy in input_copies[1:]:
        copy.wait()

    def regroup_inputs(m):
        pieces = [
            ref[16 * m : 16 * (m + 1), LANES * j : LANES * (j + 1)]
            for ref in (q_ref, k_ref, v_ref, g_ref)
            for j in range(4)
        ]
        rows = dot(swap, jnp.concatenate(pieces, axis=0)).astype(BF16)
        send_x[16 * m : 16 * (m + 1)] = rows.reshape(16, 16, LANES)

    for m in range(4):
        regroup_inputs(m)
    pl.semaphore_wait(barrier, SEQ - 1 + FILTERS + 2 - own_filter.astype(jnp.int32))

    def send_filter(step, carry):
        r = (me + step) % FILTERS
        target = CHAN * r + group
        to_self = (target == me) & (part_of == group)

        @pl.when(to_self)
        def _():
            pltpu.make_async_copy(send_f.at[r], recv_f.at[me], recv_f_sem).start()

        @pl.when(jnp.logical_not(to_self))
        def _():
            pltpu.make_async_remote_copy(
                src_ref=send_f.at[r],
                dst_ref=recv_f.at[me],
                send_sem=send_f_sem,
                recv_sem=recv_f_sem,
                device_id={"seq": target, "chan": part_of},
                device_id_type=MESH,
            ).start()

        return carry

    lax.fori_loop(0, FILTERS, send_filter, 0)

    pltpu.make_async_copy(send_x.at[channel], recv_x.at[me], recv_x_sem).start()
    def send_inputs(some):
        for dz, high, low in some:
            place = planes[dz] + highs[high]
            pltpu.make_async_remote_copy(
                src_ref=send_x.at[lows[low] * FILTERS + place // CHAN],
                dst_ref=recv_x.at[me],
                send_sem=send_x_sem,
                recv_sem=recv_x_sem,
                device_id={"seq": place + lows[low]},
                device_id_type=MESH,
            ).start()

    send_inputs(steps)

    def filter_part(index):
        return recv_f.at[pl.ds(index * FILTERS, FILTERS)]

    def share(index, peer, sem):
        pltpu.make_async_remote_copy(
            src_ref=filter_part(index),
            dst_ref=filter_part(index),
            send_sem=share_send_sem,
            recv_sem=sem,
            device_id={"chan": peer},
            device_id_type=MESH,
        ).start()

    pltpu.make_async_copy(filter_part(group), filter_part(group), recv_f_sem).wait()
    share(group, far_peer, far_sem)
    share(group, core_peer, share_recv_sem)
    pltpu.make_async_copy(filter_part(far_peer), filter_part(far_peer), far_sem).wait()
    share(far_peer, core_peer, share_recv_sem)
    three = recv_f.at[pl.ds(0, (CHAN - 1) * FILTERS)]

    for copy in taps_copies + table_copies:
        copy.wait()

    cosine, sine = twist_ref[0], twist_ref[1]

    def spectrum(outer):
        real, imag = outer[:ROWS], outer[ROWS:]
        turned = jnp.concatenate([real * cosine + imag * sine, imag * cosine - real * sine], axis=1)
        whole = table_right(*split(turned), mid_ref)
        return whole[:, :LANES], whole[:, LANES:]

    pltpu.make_async_copy(recv_x, recv_x, recv_x_sem).wait()
    sort_x = sort_matrix(16, 4, True)
    parts = []
    for m in range(4):
        got = recv_x[16 * m : 16 * (m + 1)].reshape(256, LANES)
        parts.append(dot(sort_x, got))
    query, key, value, cotangent = (
        jnp.concatenate([rows[64 * i : 64 * (i + 1)] for rows in parts], axis=0) for i in range(4)
    )

    def causal_taps(signal, taps):
        return (
            taps[0, channel] * signal + taps[1, channel] * delayed(signal, 1) + taps[2, channel] * delayed(signal, 2)
        )

    def reverse_taps(signal, taps):
        return (
            taps[0, channel] * signal + taps[1, channel] * advanced(signal, 1) + taps[2, channel] * advanced(signal, 2)
        )

    short_q = causal_taps(query, qt_ref)
    short_k = causal_taps(key, kt_ref)
    short_v = causal_taps(value, vt_ref)
    product = short_k * short_v
    grad_mixed = cotangent * short_q

    outer = table_left(first_ref, *split(jnp.concatenate([product, grad_mixed], axis=1)))
    spec[0], spec[1] = spectrum(outer[:, :LANES])
    spec[2], spec[3] = spectrum(outer[:, LANES:])

    two = recv_f.at[pl.ds(0, 2 * FILTERS)]
    pltpu.make_async_copy(two, two, share_recv_sem).wait()
    sort_f = sort_matrix(32, 2, True)
    filt_hi, filt_lo = [], []
    for m in range(2):
        got = recv_f[32 * m : 32 * (m + 1)].reshape(256, LANES)
        rows = dot(sort_f, got).astype(BF16)
        filt_hi.append(rows[:128])
        filt_lo.append(rows[128:])
    filt_re, filt_im = spectrum(
        table_left(first_ref, jnp.concatenate(filt_hi, axis=0), jnp.concatenate(filt_lo, axis=0))
    )

    def inverse(real, imag):
        back = table_right(*split(jnp.concatenate([real, imag], axis=1)), back_ref)
        real, imag = back[:, :LANES], back[:, LANES:]
        return jnp.concatenate([real * cosine - imag * sine, imag * cosine + real * sine], axis=0)

    prod_re, prod_im = spec[0], spec[1]
    fwd = inverse(filt_re * prod_re - filt_im * prod_im, filt_re * prod_im + filt_im * prod_re)
    grad_re, grad_im = spec[2], spec[3]
    bwd = inverse(filt_re * grad_re + filt_im * grad_im, filt_re * grad_im - filt_im * grad_re)
    both = table_left(last_ref, *split(jnp.concatenate([fwd, bwd], axis=1)))
    causal, backward = both[:, :LANES], both[:, LANES:]

    gain = gain_ref[channel]
    mixed = causal + gain * product
    gated = short_q * mixed
    grad_product = backward + gain * grad_mixed
    outs = [
        gated.astype(BF16),
        reverse_taps(cotangent * mixed, qt_ref).astype(BF16),
        reverse_taps(grad_product * short_v, kt_ref).astype(BF16),
        reverse_taps(grad_product * short_k, vt_ref).astype(BF16),
    ]
    sort_y = sort_matrix(16, 4, False)
    for m in range(4):
        rows = jnp.concatenate([out[64 * m : 64 * (m + 1)] for out in outs], axis=0)
        send_y[16 * m : 16 * (m + 1)] = dot(sort_y, rows).astype(BF16).reshape(16, 16, LANES)

    pltpu.make_async_copy(send_y.at[me], recv_y.at[channel], recv_y_sem).start()
    for dz, high, low in steps:
        target = planes[dz] + highs[high] + lows[low]
        pltpu.make_async_remote_copy(
            src_ref=send_y.at[target],
            dst_ref=recv_y.at[channel],
            send_sem=send_y_sem,
            recv_sem=recv_y_sem,
            device_id={"seq": target},
            device_id_type=MESH,
        ).start()

    sent = send_x.at[pl.ds(0, SEQ - 1)]
    pltpu.make_async_copy(sent, sent, send_x_sem).wait()
    pltpu.make_async_copy(three, three, share_send_sem).wait()

    @pl.when(own_filter)
    def _():
        some = send_f.at[pl.ds(0, FILTERS - 1)]
        pltpu.make_async_copy(some, some, send_f_sem).wait()

    @pl.when(jnp.logical_not(own_filter))
    def _():
        pltpu.make_async_copy(send_f, send_f, send_f_sem).wait()

    pltpu.make_async_copy(recv_y, recv_y, recv_y_sem).wait()
    sent = send_y.at[pl.ds(0, SEQ - 1)]
    pltpu.make_async_copy(sent, sent, send_y_sem).wait()


def scatter_kernel(in_ref, *refs):
    out_hbm, out_refs, out_sem = refs[:4], refs[4:8], refs[8]
    swap = swap_matrix()
    for m in range(4):
        rows = dot(swap, in_ref[16 * m : 16 * (m + 1)].reshape(256, LANES)).astype(BF16)
        for i, ref in enumerate(out_refs):
            for j in range(4):
                at = (4 * i + j) * 16
                ref[16 * m : 16 * (m + 1), LANES * j : LANES * (j + 1)] = rows[at : at + 16]
    stores = [
        pltpu.make_async_copy(ref, hbm, out_sem.at[i])
        for i, (ref, hbm) in enumerate(zip(out_refs, out_hbm))
    ]
    for store in stores:
        store.start()
    for store in stores:
        store.wait()


def body(q, k, v, long_filter, q_taps, k_taps, v_taps, gain, cotangent):
    constants = [jnp.asarray(table) for table in tables()]
    vmem = pl.BlockSpec(memory_space=pltpu.VMEM)
    anywhere = pl.BlockSpec(memory_space=pl.ANY)
    block = pltpu.VMEM((SEQ, BLOCK), BF16)
    exchange = pltpu.VMEM((SEQ, 16, LANES), BF16)
    arrived = pl.pallas_call(
        kernel,
        out_shape=jax.ShapeDtypeStruct((SEQ, 16, LANES), BF16),
        in_specs=[anywhere] * 14,
        out_specs=vmem,
        scratch_shapes=[block] * 4
        + [pltpu.VMEM((FILTERS, BLOCK), F32)]
        + [pltpu.SMEM((3, SEQ), F32)] * 3
        + [pltpu.SMEM((SEQ,), F32)]
        + [
            pltpu.VMEM((2, 512, 256), BF16),
            pltpu.VMEM((2, 256, 512), BF16),
            pltpu.VMEM((2, 256, 256), BF16),
            pltpu.VMEM((2, 256, 256), BF16),
            pltpu.VMEM((2, ROWS, LANES), F32),
            exchange,
            exchange,
            pltpu.VMEM((FILTERS, 8, LANES), BF16),
            pltpu.VMEM((SEQ, 8, LANES), BF16),
            exchange,
            pltpu.VMEM((4, ROWS, LANES), F32),
            pltpu.SemaphoreType.DMA((5,)),
            pltpu.SemaphoreType.DMA((4,)),
            pltpu.SemaphoreType.DMA((5,)),
        ]
        + [pltpu.SemaphoreType.DMA] * 9,
        compiler_params=pltpu.CompilerParams(
            collective_id=0, has_side_effects=True, vmem_limit_bytes=VMEM_LIMIT
        ),
        name="hyena",
    )(q, k, v, cotangent, long_filter, q_taps, k_taps, v_taps, gain, *constants)
    return pl.pallas_call(
        scatter_kernel,
        out_shape=[jax.ShapeDtypeStruct((SEQ, BLOCK), BF16)] * 4,
        in_specs=[vmem],
        out_specs=[anywhere] * 4,
        scratch_shapes=[block] * 4 + [pltpu.SemaphoreType.DMA((4,))],
        compiler_params=pltpu.CompilerParams(vmem_limit_bytes=VMEM_LIMIT),
        name="scatter_rows",
    )(arrived)


def solution(mesh):
    in_specs = (
        P("chan", "seq"),
        P("chan", "seq"),
        P("chan", "seq"),
        P("chan", "seq"),
        P(None, "chan"),
        P(None, "chan"),
        P(None, "chan"),
        P("chan"),
        P("chan", "seq"),
    )
    out_specs = (P("chan", "seq"),) * 4
    return jax.shard_map(body, mesh=mesh, in_specs=in_specs, out_specs=out_specs, check_vma=False)
```

```python
import functools

import jax
import jax.numpy as jnp
import ml_dtypes
import numpy as np
from jax import lax
from jax.experimental import pallas as pl
from jax.experimental.pallas import tpu as pltpu
from jax.sharding import PartitionSpec as P

SEQ = 64
CHAN = 4
BLOCK = 512
LANES = 128
ROWS = 256
FILTERS = SEQ // CHAN
FULL = 2 * ROWS * LANES
VMEM_LIMIT = 60 * 1024 * 1024

BF16 = jnp.bfloat16
F32 = jnp.float32
MESH = pl.DeviceIdType.MESH


def split_table(table):
    high = table.astype(ml_dtypes.bfloat16)
    low = (table - high.astype(np.float64)).astype(ml_dtypes.bfloat16)
    return high, low


@functools.lru_cache(maxsize=None)
def tables():
    k1 = np.arange(ROWS)
    a = np.arange(ROWS)
    b = np.arange(LANES)
    outer = 2 * np.pi * ((a[None, :] * (2 * k1[:, None] + 1)) % 1024) / 1024.0
    first = np.concatenate([np.cos(outer), -np.sin(outer)], axis=0)
    last = first.T * (2.0 / FULL)
    twist = 2 * np.pi * (b[None, :] * (2 * k1[:, None] + 1)) / (2.0 * FULL)
    inner = 2 * np.pi * ((b[None, :] * b[:, None]) % LANES) / LANES
    cosine, sine = np.cos(inner), np.sin(inner)
    mid = np.block([[cosine, -sine], [sine, cosine]])
    back = np.block([[cosine, sine], [-sine, cosine]])
    first_h, first_l = split_table(first)
    last_h, last_l = split_table(last)
    mid_h, mid_l = split_table(mid)
    back_h, back_l = split_table(back)
    return (
        np.stack([first_h, first_l]),
        np.stack([last_h, last_l]),
        np.stack([mid_h, mid_l]),
        np.stack([back_h, back_l]),
        np.stack([np.cos(twist), np.sin(twist)]).astype(np.float32),
    )


def split(value):
    high = value.astype(BF16)
    low = (value - high.astype(F32)).astype(BF16)
    return high, low


def dot(left, right):
    return jnp.dot(left, right, preferred_element_type=F32)


def table_left(table, high, low):
    table_h, table_l = table[0], table[1]
    left = jnp.concatenate([table_h, table_h, table_l], axis=1)
    return dot(left, jnp.concatenate([high, low, high], axis=0))


def table_right(high, low, table):
    table_h, table_l = table[0], table[1]
    right = jnp.concatenate([table_h, table_h, table_l], axis=0)
    return dot(jnp.concatenate([high, low, high], axis=1), right)


def swap_matrix():
    row = lax.broadcasted_iota(jnp.int32, (256, 256), 0)
    col = lax.broadcasted_iota(jnp.int32, (256, 256), 1)
    hit = (row % 16 == col // 16) & (row // 16 == col % 16)
    return jnp.where(hit, 1.0, 0.0).astype(BF16)


def sort_matrix(outer, kinds, to_kinds):
    size = outer * kinds * 4
    row = lax.broadcasted_iota(jnp.int32, (size, size), 0)
    col = lax.broadcasted_iota(jnp.int32, (size, size), 1)
    by_kind, by_shard = (row, col) if to_kinds else (col, row)
    kind = by_kind // (outer * 4)
    shard = (by_kind // 4) % outer
    hit = by_shard == shard * (kinds * 4) + kind * 4 + by_kind % 4
    return jnp.where(hit, 1.0, 0.0).astype(BF16)


def delayed(value):
    lane = lax.broadcasted_iota(jnp.int32, (ROWS, LANES), 1)
    row = lax.broadcasted_iota(jnp.int32, (ROWS, LANES), 0)
    above = jnp.where(row == 0, 0.0, pltpu.roll(value, 1, 0))
    return [
        pltpu.roll(jnp.where(lane >= LANES - steps, above, value), steps, 1) for steps in (1, 2)
    ]


def advanced(value):
    lane = lax.broadcasted_iota(jnp.int32, (ROWS, LANES), 1)
    row = lax.broadcasted_iota(jnp.int32, (ROWS, LANES), 0)
    below = jnp.where(row == ROWS - 1, 0.0, pltpu.roll(value, ROWS - 1, 0))
    return [pltpu.roll(jnp.where(lane < steps, below, value), LANES - steps, 1) for steps in (1, 2)]


def side_by_side(left, right):
    return jnp.concatenate([left, right], axis=1)


def kernel(
    q_hbm, k_hbm, v_hbm, g_hbm, filt_hbm, qt_hbm, kt_hbm, vt_hbm, gain_hbm,
    first_hbm, last_hbm, mid_hbm, back_hbm, twist_hbm,
    recv_y,
    q_ref, k_ref, v_ref, g_ref, filt_ref, qt_ref, kt_ref, vt_ref, gain_ref,
    first_ref, last_ref, mid_ref, back_ref, twist_ref,
    send_x, recv_x, send_f, recv_f, send_y, spec,
    input_sem, taps_sem, table_sem, send_x_sem, recv_x_sem, send_f_sem, recv_f_sem,
    share_send_sem, share_recv_sem, far_sem, send_y_sem, recv_y_sem,
):
    me = lax.axis_index("seq")
    group = lax.axis_index("chan")
    home, part_of = me % CHAN, me // FILTERS
    channel = home * FILTERS + me // CHAN
    core_peer, far_peer = group + 1 - 2 * (group % 2), (group + 2) % CHAN
    planes = [(me // 8 + dz) % 8 * 8 for dz in range(8)]
    highs = [(me // 4 + dx) % 2 * 4 for dx in range(2)]
    lows = [home, home + 1 - 2 * (me % 2), (home + 2) % 4, (home + 2) % 4 + 1 - 2 * (me % 2)]

    def hops(dz, high, low):
        return min(dz, 8 - dz) + (low // 2 if high == 0 else 2 - low // 2) + low % 2

    steps = [(dz, high, low) for low in range(4) for high in range(2) for dz in range(8)]
    steps = sorted(steps[1:], key=lambda step: -hops(*step))

    def copies(pairs, sems):
        return [
            pltpu.make_async_copy(source, target, sems.at[index])
            for index, (source, target) in enumerate(pairs)
        ]

    input_copies = copies(
        [(filt_hbm, filt_ref), (q_hbm, q_ref), (k_hbm, k_ref), (v_hbm, v_ref), (g_hbm, g_ref)],
        input_sem,
    )
    taps_copies = copies(
        [(qt_hbm, qt_ref), (kt_hbm, kt_ref), (vt_hbm, vt_ref), (gain_hbm, gain_ref)], taps_sem
    )
    table_copies = copies(
        [
            (first_hbm, first_ref),
            (mid_hbm, mid_ref),
            (twist_hbm, twist_ref),
            (back_hbm, back_ref),
            (last_hbm, last_ref),
        ],
        table_sem,
    )
    for copy in input_copies:
        copy.start()

    barrier = pltpu.get_barrier_semaphore()

    own_filter = (home == group) & (part_of == group)

    for step in range(1, FILTERS):
        source = group * FILTERS + (me + step) % FILTERS
        pl.semaphore_signal(
            barrier, inc=1, device_id={"seq": source, "chan": home}, device_id_type=MESH
        )

    @pl.when(jnp.logical_not(own_filter))
    def _():
        pl.semaphore_signal(
            barrier,
            inc=1,
            device_id={"seq": group * FILTERS + me % FILTERS, "chan": home},
            device_id_type=MESH,
        )

    for dz, high, low in steps:
        partner = planes[dz] + highs[high] + lows[low]
        pl.semaphore_signal(barrier, inc=1, device_id={"seq": partner}, device_id_type=MESH)
    for peer in (core_peer, far_peer):
        pl.semaphore_signal(barrier, inc=1, device_id={"chan": peer}, device_id_type=MESH)
    for copy in taps_copies + table_copies:
        copy.start()
    input_copies[0].wait()

    filt_h, filt_l = split(filt_ref[...])
    pieces = [part[:, LANES * j : LANES * (j + 1)] for part in (filt_h, filt_l) for j in range(4)]
    row = lax.broadcasted_iota(jnp.int32, (128, 128), 0)
    col = lax.broadcasted_iota(jnp.int32, (128, 128), 1)
    regroup = jnp.where((row % 8 == col // 16) & (row // 8 == col % 16), 1.0, 0.0).astype(BF16)
    send_f[...] = dot(regroup, jnp.concatenate(pieces, axis=0)).astype(BF16).reshape(FILTERS, 8, LANES)
    swap = swap_matrix()
    for copy in input_copies[1:]:
        copy.wait()

    def gather(m):
        return jnp.concatenate(
            [
                ref[16 * m : 16 * (m + 1), LANES * j : LANES * (j + 1)]
                for ref in (q_ref, k_ref, v_ref, g_ref)
                for j in range(4)
            ],
            axis=0,
        )

    for m in (0, 2):
        rows = dot(swap, side_by_side(gather(m), gather(m + 1))).astype(BF16)
        send_x[16 * m : 16 * (m + 1)] = rows[:, :LANES].reshape(16, 16, LANES)
        send_x[16 * (m + 1) : 16 * (m + 2)] = rows[:, LANES:].reshape(16, 16, LANES)

    pl.semaphore_wait(barrier, SEQ - 1 + FILTERS + 2 - own_filter.astype(jnp.int32))

    def send_filter(r):
        pltpu.make_async_remote_copy(
            src_ref=send_f.at[r],
            dst_ref=recv_f.at[me],
            send_sem=send_f_sem,
            recv_sem=recv_f_sem,
            device_id={"seq": CHAN * r + group, "chan": part_of},
            device_id_type=MESH,
        ).start()

    for step in sorted(range(1, FILTERS), key=lambda step: -min(step, FILTERS - step)):
        send_filter((me // CHAN + step) % FILTERS)

    @pl.when(own_filter)
    def _():
        pltpu.make_async_copy(send_f.at[me // CHAN], recv_f.at[me], recv_f_sem).start()

    @pl.when(jnp.logical_not(own_filter))
    def _():
        send_filter(me // CHAN)

    pltpu.make_async_copy(send_x.at[channel], recv_x.at[me], recv_x_sem).start()
    def send_inputs(some):
        for dz, high, low in some:
            place = planes[dz] + highs[high]
            pltpu.make_async_remote_copy(
                src_ref=send_x.at[lows[low] * FILTERS + place // CHAN],
                dst_ref=recv_x.at[me],
                send_sem=send_x_sem,
                recv_sem=recv_x_sem,
                device_id={"seq": place + lows[low]},
                device_id_type=MESH,
            ).start()

    send_inputs(steps)

    def filter_part(index):
        return recv_f.at[pl.ds(index * FILTERS, FILTERS)]

    def share(index, peer, sem):
        pltpu.make_async_remote_copy(
            src_ref=filter_part(index),
            dst_ref=filter_part(index),
            send_sem=share_send_sem,
            recv_sem=sem,
            device_id={"chan": peer},
            device_id_type=MESH,
        ).start()

    pltpu.make_async_copy(filter_part(group), filter_part(group), recv_f_sem).wait()
    share(group, far_peer, far_sem)
    share(group, core_peer, share_recv_sem)
    pltpu.make_async_copy(filter_part(far_peer), filter_part(far_peer), far_sem).wait()
    share(far_peer, core_peer, share_recv_sem)
    three = recv_f.at[pl.ds(0, (CHAN - 1) * FILTERS)]

    for copy in taps_copies + table_copies:
        copy.wait()

    cosine, sine = twist_ref[0], twist_ref[1]

    def twist(real, imag):
        return side_by_side(real * cosine + imag * sine, imag * cosine - real * sine)

    def untwist(back):
        real, imag = back[:, :LANES], back[:, LANES:]
        return jnp.concatenate([real * cosine - imag * sine, imag * cosine + real * sine], axis=0)

    pltpu.make_async_copy(recv_x, recv_x, recv_x_sem).wait()
    sort_x = sort_matrix(16, 4, True)
    parts = []
    for m in (0, 2):
        pair = [recv_x[16 * n : 16 * (n + 1)].reshape(256, LANES) for n in (m, m + 1)]
        rows = dot(sort_x, side_by_side(*pair))
        parts += [rows[:, :LANES], rows[:, LANES:]]
    query, key, value, cotangent = (
        jnp.concatenate([rows[64 * i : 64 * (i + 1)] for rows in parts], axis=0) for i in range(4)
    )

    def short_filter(signal, taps, near, far):
        return taps[0, channel] * signal + taps[1, channel] * near + taps[2, channel] * far

    def causal_taps(signal, taps):
        return short_filter(signal, taps, *delayed(signal))

    def reverse_taps(signal, taps):
        return short_filter(signal, taps, *advanced(signal))

    short_q = causal_taps(query, qt_ref)
    short_k = causal_taps(key, kt_ref)
    short_v = causal_taps(value, vt_ref)
    product = short_k * short_v
    grad_mixed = cotangent * short_q

    outer = table_left(first_ref, *split(jnp.concatenate([product, grad_mixed], axis=1)))
    turned = jnp.concatenate(
        [
            twist(outer[:ROWS, :LANES], outer[ROWS:, :LANES]),
            twist(outer[:ROWS, LANES:], outer[ROWS:, LANES:]),
        ],
        axis=0,
    )
    spec[...] = table_right(*split(turned), mid_ref)

    two = recv_f.at[pl.ds(0, 2 * FILTERS)]
    pltpu.make_async_copy(two, two, share_recv_sem).wait()
    sort_f = sort_matrix(32, 2, True)
    pair = [recv_f[32 * m : 32 * (m + 1)].reshape(256, LANES) for m in range(2)]
    rows = dot(sort_f, side_by_side(*pair)).astype(BF16)
    outer = table_left(
        first_ref,
        jnp.concatenate([rows[:128, :LANES], rows[:128, LANES:]], axis=0),
        jnp.concatenate([rows[128:, :LANES], rows[128:, LANES:]], axis=0),
    )
    filt = table_right(*split(twist(outer[:ROWS], outer[ROWS:])), mid_ref)
    filt_re, filt_im = filt[:, :LANES], filt[:, LANES:]
    prod_re, prod_im = spec[:ROWS, :LANES], spec[:ROWS, LANES:]
    grad_re, grad_im = spec[ROWS:, :LANES], spec[ROWS:, LANES:]
    both = jnp.concatenate(
        [
            side_by_side(
                filt_re * prod_re - filt_im * prod_im, filt_re * prod_im + filt_im * prod_re
            ),
            side_by_side(
                filt_re * grad_re + filt_im * grad_im, filt_re * grad_im - filt_im * grad_re
            ),
        ],
        axis=0,
    )
    back = table_right(*split(both), back_ref)
    both = side_by_side(untwist(back[:ROWS]), untwist(back[ROWS:]))
    both = table_left(last_ref, *split(both))
    causal, backward = both[:, :LANES], both[:, LANES:]

    gain = gain_ref[channel]
    mixed = causal + gain * product
    gated = short_q * mixed
    grad_product = backward + gain * grad_mixed
    outs = [
        gated.astype(BF16),
        reverse_taps(cotangent * mixed, qt_ref).astype(BF16),
        reverse_taps(grad_product * short_v, kt_ref).astype(BF16),
        reverse_taps(grad_product * short_k, vt_ref).astype(BF16),
    ]
    sort_y = sort_matrix(16, 4, False)

    def chunk(m):
        return jnp.concatenate([out[64 * m : 64 * (m + 1)] for out in outs], axis=0)

    for m in (0, 2):
        rows = dot(sort_y, side_by_side(chunk(m), chunk(m + 1))).astype(BF16)
        send_y[16 * m : 16 * (m + 1)] = rows[:, :LANES].reshape(16, 16, LANES)
        send_y[16 * (m + 1) : 16 * (m + 2)] = rows[:, LANES:].reshape(16, 16, LANES)

    pltpu.make_async_copy(send_y.at[me], recv_y.at[channel], recv_y_sem).start()
    for dz, high, low in steps:
        target = planes[dz] + highs[high] + lows[low]
        pltpu.make_async_remote_copy(
            src_ref=send_y.at[target],
            dst_ref=recv_y.at[channel],
            send_sem=send_y_sem,
            recv_sem=recv_y_sem,
            device_id={"seq": target},
            device_id_type=MESH,
        ).start()

    sent = send_x.at[pl.ds(0, SEQ - 1)]
    pltpu.make_async_copy(sent, sent, send_x_sem).wait()
    pltpu.make_async_copy(three, three, share_send_sem).wait()

    @pl.when(own_filter)
    def _():
        some = send_f.at[pl.ds(0, FILTERS - 1)]
        pltpu.make_async_copy(some, some, send_f_sem).wait()

    @pl.when(jnp.logical_not(own_filter))
    def _():
        pltpu.make_async_copy(send_f, send_f, send_f_sem).wait()

    pltpu.make_async_copy(recv_y, recv_y, recv_y_sem).wait()
    sent = send_y.at[pl.ds(0, SEQ - 1)]
    pltpu.make_async_copy(sent, sent, send_y_sem).wait()


def scatter_kernel(in_hbm, *refs):
    out_hbm, in_ref, out_refs, in_sem, out_sem = refs[:4], refs[4], refs[5:9], refs[9], refs[10]
    load = pltpu.make_async_copy(in_hbm, in_ref, in_sem)
    load.start()
    swap = swap_matrix()
    load.wait()
    for m in range(4):
        rows = dot(swap, in_ref[16 * m : 16 * (m + 1)].reshape(256, LANES)).astype(BF16)
        for i, ref in enumerate(out_refs):
            for j in range(4):
                at = (4 * i + j) * 16
                ref[16 * m : 16 * (m + 1), LANES * j : LANES * (j + 1)] = rows[at : at + 16]
    stores = [
        pltpu.make_async_copy(ref, hbm, out_sem.at[i])
        for i, (ref, hbm) in enumerate(zip(out_refs, out_hbm))
    ]
    for store in stores:
        store.start()
    for store in stores:
        store.wait()


def body(q, k, v, long_filter, q_taps, k_taps, v_taps, gain, cotangent):
    constants = [jnp.asarray(table) for table in tables()]
    hbm = pl.BlockSpec(memory_space=pltpu.HBM)
    block = pltpu.VMEM((SEQ, BLOCK), BF16)
    exchange = pltpu.VMEM((SEQ, 16, LANES), BF16)
    arrived = pl.pallas_call(
        kernel,
        out_shape=jax.ShapeDtypeStruct((SEQ, 16, LANES), BF16),
        in_specs=[hbm] * 14,
        out_specs=hbm,
        scratch_shapes=[block] * 4
        + [pltpu.VMEM((FILTERS, BLOCK), F32)]
        + [pltpu.SMEM((3, SEQ), F32)] * 3
        + [pltpu.SMEM((SEQ,), F32)]
        + [
            pltpu.VMEM((2, 512, 256), BF16),
            pltpu.VMEM((2, 256, 512), BF16),
            pltpu.VMEM((2, 256, 256), BF16),
            pltpu.VMEM((2, 256, 256), BF16),
            pltpu.VMEM((2, ROWS, LANES), F32),
            exchange,
            exchange,
            pltpu.VMEM((FILTERS, 8, LANES), BF16),
            pltpu.VMEM((SEQ, 8, LANES), BF16),
            exchange,
            pltpu.VMEM((2 * ROWS, 2 * LANES), F32),
            pltpu.SemaphoreType.DMA((5,)),
            pltpu.SemaphoreType.DMA((4,)),
            pltpu.SemaphoreType.DMA((5,)),
        ]
        + [pltpu.SemaphoreType.DMA] * 9,
        compiler_params=pltpu.CompilerParams(
            collective_id=0, has_side_effects=True, vmem_limit_bytes=VMEM_LIMIT
        ),
        name="hyena",
    )(q, k, v, cotangent, long_filter, q_taps, k_taps, v_taps, gain, *constants)
    return pl.pallas_call(
        scatter_kernel,
        out_shape=[jax.ShapeDtypeStruct((SEQ, BLOCK), BF16)] * 4,
        in_specs=[hbm],
        out_specs=[hbm] * 4,
        scratch_shapes=[exchange]
        + [block] * 4
        + [pltpu.SemaphoreType.DMA, pltpu.SemaphoreType.DMA((4,))],
        compiler_params=pltpu.CompilerParams(vmem_limit_bytes=VMEM_LIMIT),
        name="scatter_rows",
    )(arrived)


def solution(mesh):
    in_specs = (
        P("chan", "seq"),
        P("chan", "seq"),
        P("chan", "seq"),
        P("chan", "seq"),
        P(None, "chan"),
        P(None, "chan"),
        P(None, "chan"),
        P("chan"),
        P("chan", "seq"),
    )
    out_specs = (P("chan", "seq"),) * 4
    return jax.shard_map(body, mesh=mesh, in_specs=in_specs, out_specs=out_specs, check_vma=False)
```

```python
import functools

import jax
import jax.numpy as jnp
import ml_dtypes
import numpy as np
from jax import lax
from jax.experimental import pallas as pl
from jax.experimental.pallas import tpu as pltpu
from jax.sharding import PartitionSpec as P

SEQ = 64
CHAN = 4
BLOCK = 512
LANES = 128
ROWS = 256
FILTERS = SEQ // CHAN
FULL = 2 * ROWS * LANES
VMEM_LIMIT = 60 * 1024 * 1024

BF16 = jnp.bfloat16
F32 = jnp.float32
MESH = pl.DeviceIdType.MESH


def split_table(table):
    high = table.astype(ml_dtypes.bfloat16)
    low = (table - high.astype(np.float64)).astype(ml_dtypes.bfloat16)
    return high, low


@functools.lru_cache(maxsize=None)
def tables():
    k1 = np.arange(ROWS)
    a = np.arange(ROWS)
    b = np.arange(LANES)
    outer = 2 * np.pi * ((a[None, :] * (2 * k1[:, None] + 1)) % 1024) / 1024.0
    first = np.concatenate([np.cos(outer), -np.sin(outer)], axis=0)
    last = first.T * (2.0 / FULL)
    twist = 2 * np.pi * (b[None, :] * (2 * k1[:, None] + 1)) / (2.0 * FULL)
    inner = 2 * np.pi * ((b[None, :] * b[:, None]) % LANES) / LANES
    cosine, sine = np.cos(inner), np.sin(inner)
    mid = np.block([[cosine, -sine], [sine, cosine]])
    back = np.block([[cosine, sine], [-sine, cosine]])
    first_h, first_l = split_table(first)
    last_h, last_l = split_table(last)
    mid_h, mid_l = split_table(mid)
    back_h, back_l = split_table(back)
    return (
        np.stack([first_h, first_l]),
        np.stack([last_h, last_l]),
        np.stack([mid_h, mid_l]),
        np.stack([back_h, back_l]),
        np.stack([np.cos(twist), np.sin(twist)]).astype(np.float32),
    )


def split(value):
    high = value.astype(BF16)
    low = (value - high.astype(F32)).astype(BF16)
    return high, low


def dot(left, right):
    return jnp.dot(left, right, preferred_element_type=F32)


def table_left(table, high, low):
    table_h, table_l = table[0], table[1]
    left = jnp.concatenate([table_h, table_h, table_l], axis=1)
    return dot(left, jnp.concatenate([high, low, high], axis=0))


def table_right(high, low, table):
    table_h, table_l = table[0], table[1]
    right = jnp.concatenate([table_h, table_h, table_l], axis=0)
    return dot(jnp.concatenate([high, low, high], axis=1), right)


def swap_matrix(outer):
    row = lax.broadcasted_iota(jnp.int32, (256, 256), 0)
    col = lax.broadcasted_iota(jnp.int32, (256, 256), 1)
    inner = 256 // outer
    return jnp.where(col == row % inner * outer + row // inner, 1.0, 0.0).astype(BF16)


def sort_matrix(outer, kinds, to_kinds):
    size = outer * kinds * 4
    row = lax.broadcasted_iota(jnp.int32, (size, size), 0)
    col = lax.broadcasted_iota(jnp.int32, (size, size), 1)
    by_kind, by_shard = (row, col) if to_kinds else (col, row)
    kind = by_kind // (outer * 4)
    shard = (by_kind // 4) % outer
    hit = by_shard == shard * (kinds * 4) + kind * 4 + by_kind % 4
    return jnp.where(hit, 1.0, 0.0).astype(BF16)


def delayed(value):
    lane = lax.broadcasted_iota(jnp.int32, (ROWS, LANES), 1)
    row = lax.broadcasted_iota(jnp.int32, (ROWS, LANES), 0)
    above = jnp.where(row == 0, 0.0, pltpu.roll(value, 1, 0))
    return [
        pltpu.roll(jnp.where(lane >= LANES - steps, above, value), steps, 1) for steps in (1, 2)
    ]


def advanced(value):
    lane = lax.broadcasted_iota(jnp.int32, (ROWS, LANES), 1)
    row = lax.broadcasted_iota(jnp.int32, (ROWS, LANES), 0)
    below = jnp.where(row == ROWS - 1, 0.0, pltpu.roll(value, ROWS - 1, 0))
    return [pltpu.roll(jnp.where(lane < steps, below, value), LANES - steps, 1) for steps in (1, 2)]


def put_groups(target, rows):
    target[0:32] = rows[:, :LANES].astype(BF16).reshape(32, 8, LANES)
    target[32:64] = rows[:, LANES:].astype(BF16).reshape(32, 8, LANES)


def get_groups(source):
    return side_by_side(*[source[32 * m : 32 * (m + 1)].reshape(256, LANES) for m in range(2)])


def stack_groups(rows):
    return [
        jnp.concatenate([rows[at : at + 128, :LANES], rows[at : at + 128, LANES:]], axis=0)
        for at in (0, 128)
    ]


def side_by_side(left, right):
    return jnp.concatenate([left, right], axis=1)


def kernel(
    q_hbm, k_hbm, v_hbm, g_hbm, filt_hbm, qt_hbm, kt_hbm, vt_hbm, gain_hbm,
    first_hbm, last_hbm, mid_hbm, back_hbm, twist_hbm,
    recv_c, recv_d,
    q_ref, k_ref, v_ref, g_ref, filt_ref, qt_ref, kt_ref, vt_ref, gain_ref,
    first_ref, last_ref, mid_ref, back_ref, twist_ref,
    send_a, recv_a, send_b, recv_b, send_f, recv_f, send_c, send_d,
    filt_spec, short_k, short_v, mixed_ref, grad_ref,
    input_sem, taps_sem, table_sem,
    in_a_sem, in_b_sem, out_c_sem, out_d_sem,
    send_f_sem, recv_f_sem, share_send_sem, share_recv_sem,
):
    me = lax.axis_index("seq")
    group = lax.axis_index("chan")
    home, core = me % CHAN, group % 2
    own_filter = (home == group) & (me // (2 * FILTERS) == core)
    half = me // (2 * FILTERS)
    channel = home * FILTERS + me // CHAN
    core_peer = group + 1 - 2 * core
    planes = [(me // 8 + dz) % 8 * 8 for dz in range(8)]
    highs = [(me // 4 + dx) % 2 * 4 for dx in range(2)]
    lows = [home, home + 1 - 2 * (me % 2), (home + 2) % 4, (home + 2) % 4 + 1 - 2 * (me % 2)]

    def hops(dz, high, low):
        return min(dz, 8 - dz) + (low // 2 if high == 0 else 2 - low // 2) + low % 2

    steps = [(dz, high, low) for low in range(4) for high in range(2) for dz in range(8)]
    steps = sorted(steps[1:], key=lambda step: -hops(*step))

    def copies(pairs, sems):
        return [
            pltpu.make_async_copy(source, target, sems.at[index])
            for index, (source, target) in enumerate(pairs)
        ]

    input_copies = copies(
        [(filt_hbm, filt_ref), (q_hbm, q_ref), (k_hbm, k_ref), (v_hbm, v_ref), (g_hbm, g_ref)],
        input_sem,
    )
    taps_copies = copies(
        [(qt_hbm, qt_ref), (kt_hbm, kt_ref), (vt_hbm, vt_ref), (gain_hbm, gain_ref)], taps_sem
    )
    table_copies = copies(
        [
            (first_hbm, first_ref),
            (mid_hbm, mid_ref),
            (twist_hbm, twist_ref),
            (back_hbm, back_ref),
            (last_hbm, last_ref),
        ],
        table_sem,
    )
    for copy in input_copies:
        copy.start()

    barrier = pltpu.get_barrier_semaphore()


    for step in range(1, 2 * FILTERS):
        source = core * 2 * FILTERS + (me + step) % (2 * FILTERS)
        pl.semaphore_signal(
            barrier, inc=1, device_id={"seq": source, "chan": home}, device_id_type=MESH
        )

    @pl.when(jnp.logical_not(own_filter))
    def _():
        source = core * 2 * FILTERS + me % (2 * FILTERS)
        pl.semaphore_signal(
            barrier, inc=1, device_id={"seq": source, "chan": home}, device_id_type=MESH
        )

    for dz, high, low in steps:
        partner = planes[dz] + highs[high] + lows[low]
        pl.semaphore_signal(barrier, inc=1, device_id={"seq": partner}, device_id_type=MESH)
    pl.semaphore_signal(barrier, inc=1, device_id={"chan": core_peer}, device_id_type=MESH)
    for copy in taps_copies + table_copies:
        copy.start()
    input_copies[0].wait()

    filt_h, filt_l = split(filt_ref[...])
    pieces = [part[:, LANES * j : LANES * (j + 1)] for part in (filt_h, filt_l) for j in range(4)]
    row = lax.broadcasted_iota(jnp.int32, (128, 128), 0)
    col = lax.broadcasted_iota(jnp.int32, (128, 128), 1)
    regroup = jnp.where((row % 8 == col // 16) & (row // 8 == col % 16), 1.0, 0.0).astype(BF16)
    send_f[...] = dot(regroup, jnp.concatenate(pieces, axis=0)).astype(BF16).reshape(FILTERS, 8, LANES)
    swap = swap_matrix(32)
    for copy in input_copies[1:]:
        copy.wait()
    for target, refs in ((send_a, (k_ref, v_ref)), (send_b, (q_ref, g_ref))):
        groups = [
            jnp.concatenate(
                [
                    ref[32 * m : 32 * (m + 1), LANES * j : LANES * (j + 1)]
                    for ref in refs
                    for j in range(4)
                ],
                axis=0,
            )
            for m in range(2)
        ]
        put_groups(target, dot(swap, side_by_side(*groups)))

    pl.semaphore_wait(barrier, SEQ - 1 + 2 * FILTERS + 1 - own_filter.astype(jnp.int32))

    def send_filter(r, far):
        pltpu.make_async_remote_copy(
            src_ref=send_f.at[r],
            dst_ref=recv_f.at[me],
            send_sem=send_f_sem,
            recv_sem=recv_f_sem,
            device_id={"seq": CHAN * r + group, "chan": (group // 2 + far) % 2 * 2 + half},
            device_id_type=MESH,
        ).start()

    for step in sorted(range(FILTERS), key=lambda step: -min(step, FILTERS - step)):
        send_filter((me // CHAN + step) % FILTERS, 1)
        if step > 0:
            send_filter((me // CHAN + step) % FILTERS, 0)

    @pl.when(own_filter)
    def _():
        pltpu.make_async_copy(send_f.at[me // CHAN], recv_f.at[me], recv_f_sem).start()

    @pl.when(jnp.logical_not(own_filter))
    def _():
        send_filter(me // CHAN, 0)

    def send_inputs(source, target, sems):
        pltpu.make_async_copy(source.at[channel], target.at[me], sems.at[1]).start()
        for dz, high, low in steps:
            place = planes[dz] + highs[high]
            pltpu.make_async_remote_copy(
                src_ref=source.at[lows[low] * FILTERS + place // CHAN],
                dst_ref=target.at[me],
                send_sem=sems.at[0],
                recv_sem=sems.at[1],
                device_id={"seq": place + lows[low]},
                device_id_type=MESH,
            ).start()

    def send_outputs(source, target, sems):
        pltpu.make_async_copy(source.at[me], target.at[channel], sems.at[1]).start()
        for dz, high, low in steps:
            place = planes[dz] + highs[high] + lows[low]
            pltpu.make_async_remote_copy(
                src_ref=source.at[place],
                dst_ref=target.at[channel],
                send_sem=sems.at[0],
                recv_sem=sems.at[1],
                device_id={"seq": place},
                device_id_type=MESH,
            ).start()

    send_inputs(send_a, recv_a, in_a_sem)
    send_inputs(send_b, recv_b, in_b_sem)

    own_half = recv_f.at[pl.ds(core * 2 * FILTERS, 2 * FILTERS)]
    pltpu.make_async_copy(own_half, own_half, recv_f_sem).wait()
    pltpu.make_async_remote_copy(
        src_ref=own_half,
        dst_ref=own_half,
        send_sem=share_send_sem,
        recv_sem=share_recv_sem,
        device_id={"chan": core_peer},
        device_id_type=MESH,
    ).start()

    for copy in taps_copies + table_copies:
        copy.wait()

    cosine, sine = twist_ref[0], twist_ref[1]

    def twist(real, imag):
        return side_by_side(real * cosine + imag * sine, imag * cosine - real * sine)

    def untwist(back):
        real, imag = back[:, :LANES], back[:, LANES:]
        return jnp.concatenate([real * cosine - imag * sine, imag * cosine + real * sine], axis=0)

    def short_filter(signal, taps, near, far):
        return taps[0, channel] * signal + taps[1, channel] * near + taps[2, channel] * far

    def causal_taps(signal, taps):
        return short_filter(signal, taps, *delayed(signal))

    def reverse_taps(signal, taps):
        return short_filter(signal, taps, *advanced(signal))

    sort_in = sort_matrix(32, 2, True)
    sort_out = sort_matrix(32, 2, False)
    gain = gain_ref[channel]

    pltpu.make_async_copy(recv_a, recv_a, in_a_sem.at[1]).wait()
    key, value = stack_groups(dot(sort_in, get_groups(recv_a)))
    short_k[...] = causal_taps(key, kt_ref)
    short_v[...] = causal_taps(value, vt_ref)
    product = short_k[...] * short_v[...]
    prod_h, prod_l = split(product)
    pltpu.make_async_copy(own_half, own_half, share_recv_sem).wait()
    filt_h, filt_l = stack_groups(dot(sort_in, get_groups(recv_f)).astype(BF16))
    outer = table_left(first_ref, side_by_side(filt_h, prod_h), side_by_side(filt_l, prod_l))
    turned = jnp.concatenate(
        [
            twist(outer[:ROWS, :LANES], outer[ROWS:, :LANES]),
            twist(outer[:ROWS, LANES:], outer[ROWS:, LANES:]),
        ],
        axis=0,
    )
    spec = table_right(*split(turned), mid_ref)
    filt_re, filt_im = spec[:ROWS, :LANES], spec[:ROWS, LANES:]
    prod_re, prod_im = spec[ROWS:, :LANES], spec[ROWS:, LANES:]
    filt_spec[...] = spec[:ROWS]

    def inverse(real, imag):
        back = table_right(*split(side_by_side(real, imag)), back_ref)
        return table_left(last_ref, *split(untwist(back)))

    causal = inverse(filt_re * prod_re - filt_im * prod_im, filt_re * prod_im + filt_im * prod_re)
    mixed_ref[...] = causal + gain * product

    pltpu.make_async_copy(recv_b, recv_b, in_b_sem.at[1]).wait()
    query, cotangent = stack_groups(dot(sort_in, get_groups(recv_b)))
    short_q = causal_taps(query, qt_ref)
    mixed = mixed_ref[...]
    grad_ref[...] = cotangent * short_q

    def leave(target, first, second):
        first, second = first.astype(BF16), second.astype(BF16)
        groups = [
            jnp.concatenate([first[at : at + 128], second[at : at + 128]], axis=0)
            for at in (0, 128)
        ]
        put_groups(target, dot(sort_out, side_by_side(*groups)))

    leave(send_c, short_q * mixed, reverse_taps(cotangent * mixed, qt_ref))
    send_outputs(send_c, recv_c, out_c_sem)

    grad_mixed = grad_ref[...]
    outer = table_left(first_ref, *split(grad_mixed))
    spec = table_right(*split(twist(outer[:ROWS], outer[ROWS:])), mid_ref)
    grad_re, grad_im = spec[:, :LANES], spec[:, LANES:]
    filt_re, filt_im = filt_spec[:, :LANES], filt_spec[:, LANES:]
    backward = inverse(
        filt_re * grad_re + filt_im * grad_im, filt_re * grad_im - filt_im * grad_re
    )
    grad_product = backward + gain * grad_mixed
    leave(
        send_d,
        reverse_taps(grad_product * short_v[...], kt_ref),
        reverse_taps(grad_product * short_k[...], vt_ref),
    )
    send_outputs(send_d, recv_d, out_d_sem)

    for source, sems in (
        (send_a, in_a_sem), (send_b, in_b_sem), (send_c, out_c_sem), (send_d, out_d_sem)
    ):
        sent = source.at[pl.ds(0, SEQ - 1)]
        pltpu.make_async_copy(sent, sent, sems.at[0]).wait()
    pltpu.make_async_copy(own_half, own_half, share_send_sem).wait()
    pltpu.make_async_copy(send_f, send_f, send_f_sem).wait()

    @pl.when(own_filter)
    def _():
        some = send_f.at[pl.ds(0, FILTERS - 1)]
        pltpu.make_async_copy(some, some, send_f_sem).wait()

    @pl.when(jnp.logical_not(own_filter))
    def _():
        pltpu.make_async_copy(send_f, send_f, send_f_sem).wait()

    pltpu.make_async_copy(recv_c, recv_c, out_c_sem.at[1]).wait()
    pltpu.make_async_copy(recv_d, recv_d, out_d_sem.at[1]).wait()


def scatter_kernel(c_hbm, d_hbm, *refs):
    out_hbm, in_refs, out_refs, in_sem, out_sem = refs[:4], refs[4:6], refs[6:10], refs[10], refs[11]
    loads = [
        pltpu.make_async_copy(hbm, ref, in_sem.at[i])
        for i, (hbm, ref) in enumerate(zip((c_hbm, d_hbm), in_refs))
    ]
    for load in loads:
        load.start()
    swap = swap_matrix(8)
    stores = []
    for n in range(2):
        loads[n].wait()
        rows = dot(swap, get_groups(in_refs[n])).astype(BF16)
        for i in range(2):
            ref = out_refs[2 * n + i]
            for j in range(4):
                at = (4 * i + j) * 32
                for m in range(2):
                    ref[32 * m : 32 * (m + 1), LANES * j : LANES * (j + 1)] = rows[
                        at : at + 32, LANES * m : LANES * (m + 1)
                    ]
            stores.append(pltpu.make_async_copy(ref, out_hbm[2 * n + i], out_sem.at[2 * n + i]))
            stores[-1].start()
    for store in stores:
        store.wait()


def body(q, k, v, long_filter, q_taps, k_taps, v_taps, gain, cotangent):
    constants = [jnp.asarray(table) for table in tables()]
    hbm = pl.BlockSpec(memory_space=pltpu.HBM)
    block = pltpu.VMEM((SEQ, BLOCK), BF16)
    wave = pltpu.VMEM((SEQ, 8, LANES), BF16)
    signal = pltpu.VMEM((ROWS, LANES), F32)
    arrived = pl.pallas_call(
        kernel,
        out_shape=[jax.ShapeDtypeStruct((SEQ, 8, LANES), BF16)] * 2,
        in_specs=[hbm] * 14,
        out_specs=[hbm] * 2,
        scratch_shapes=[block] * 4
        + [pltpu.VMEM((FILTERS, BLOCK), F32)]
        + [pltpu.SMEM((3, SEQ), F32)] * 3
        + [pltpu.SMEM((SEQ,), F32)]
        + [
            pltpu.VMEM((2, 512, 256), BF16),
            pltpu.VMEM((2, 256, 512), BF16),
            pltpu.VMEM((2, 256, 256), BF16),
            pltpu.VMEM((2, 256, 256), BF16),
            pltpu.VMEM((2, ROWS, LANES), F32),
            wave,
            wave,
            wave,
            wave,
            pltpu.VMEM((FILTERS, 8, LANES), BF16),
            wave,
            wave,
            wave,
            pltpu.VMEM((ROWS, 2 * LANES), F32),
        ]
        + [signal] * 4
        + [
            pltpu.SemaphoreType.DMA((5,)),
            pltpu.SemaphoreType.DMA((4,)),
            pltpu.SemaphoreType.DMA((5,)),
        ]
        + [pltpu.SemaphoreType.DMA((2,))] * 4
        + [pltpu.SemaphoreType.DMA] * 4,
        compiler_params=pltpu.CompilerParams(
            collective_id=0, has_side_effects=True, vmem_limit_bytes=VMEM_LIMIT
        ),
        name="hyena",
    )(q, k, v, cotangent, long_filter, q_taps, k_taps, v_taps, gain, *constants)
    return pl.pallas_call(
        scatter_kernel,
        out_shape=[jax.ShapeDtypeStruct((SEQ, BLOCK), BF16)] * 4,
        in_specs=[hbm] * 2,
        out_specs=[hbm] * 4,
        scratch_shapes=[wave] * 2
        + [block] * 4
        + [pltpu.SemaphoreType.DMA((2,)), pltpu.SemaphoreType.DMA((4,))],
        compiler_params=pltpu.CompilerParams(vmem_limit_bytes=VMEM_LIMIT),
        name="scatter_rows",
    )(*arrived)


def solution(mesh):
    in_specs = (
        P("chan", "seq"),
        P("chan", "seq"),
        P("chan", "seq"),
        P("chan", "seq"),
        P(None, "chan"),
        P(None, "chan"),
        P(None, "chan"),
        P("chan"),
        P("chan", "seq"),
    )
    out_specs = (P("chan", "seq"),) * 4
    return jax.shard_map(body, mesh=mesh, in_specs=in_specs, out_specs=out_specs, check_vma=False)
```

```python
import functools

import jax
import jax.numpy as jnp
import ml_dtypes
import numpy as np
from jax import lax
from jax.experimental import pallas as pl
from jax.experimental.pallas import tpu as pltpu
from jax.sharding import PartitionSpec as P

SEQ = 64
CHAN = 4
BLOCK = 512
LANES = 128
ROWS = 256
FILTERS = SEQ // CHAN
FULL = 2 * ROWS * LANES
VMEM_LIMIT = 60 * 1024 * 1024

BF16 = jnp.bfloat16
F32 = jnp.float32
MESH = pl.DeviceIdType.MESH


def split_table(table):
    high = table.astype(ml_dtypes.bfloat16)
    low = (table - high.astype(np.float64)).astype(ml_dtypes.bfloat16)
    return high, low


@functools.lru_cache(maxsize=None)
def tables():
    k1 = np.arange(ROWS)
    a = np.arange(ROWS)
    b = np.arange(LANES)
    outer = 2 * np.pi * ((a[None, :] * (2 * k1[:, None] + 1)) % 1024) / 1024.0
    first = np.concatenate([np.cos(outer), -np.sin(outer)], axis=0)
    last = first.T * (2.0 / FULL)
    twist = 2 * np.pi * (b[None, :] * (2 * k1[:, None] + 1)) / (2.0 * FULL)
    inner = 2 * np.pi * ((b[None, :] * b[:, None]) % LANES) / LANES
    cosine, sine = np.cos(inner), np.sin(inner)
    mid = np.block([[cosine, -sine], [sine, cosine]])
    back = np.block([[cosine, sine], [-sine, cosine]])
    first_h, first_l = split_table(first)
    last_h, last_l = split_table(last)
    mid_h, mid_l = split_table(mid)
    back_h, back_l = split_table(back)
    return (
        np.stack([first_h, first_l]),
        np.stack([last_h, last_l]),
        np.stack([mid_h, mid_l]),
        np.stack([back_h, back_l]),
        np.stack([np.cos(twist), np.sin(twist)]).astype(np.float32),
    )


def split(value):
    high = value.astype(BF16)
    low = (value - high.astype(F32)).astype(BF16)
    return high, low


def dot(left, right):
    return jnp.dot(left, right, preferred_element_type=F32)


def table_left(table, high, low):
    table_h, table_l = table[0], table[1]
    left = jnp.concatenate([table_h, table_h, table_l], axis=1)
    return dot(left, jnp.concatenate([high, low, high], axis=0))


def table_right(high, low, table):
    table_h, table_l = table[0], table[1]
    right = jnp.concatenate([table_h, table_h, table_l], axis=0)
    return dot(jnp.concatenate([high, low, high], axis=1), right)


def swap_matrix(outer):
    row = lax.broadcasted_iota(jnp.int32, (256, 256), 0)
    col = lax.broadcasted_iota(jnp.int32, (256, 256), 1)
    inner = 256 // outer
    return jnp.where(col == row % inner * outer + row // inner, 1.0, 0.0).astype(BF16)


def sort_matrix(outer, kinds, to_kinds):
    size = outer * kinds * 4
    row = lax.broadcasted_iota(jnp.int32, (size, size), 0)
    col = lax.broadcasted_iota(jnp.int32, (size, size), 1)
    by_kind, by_shard = (row, col) if to_kinds else (col, row)
    kind = by_kind // (outer * 4)
    shard = (by_kind // 4) % outer
    hit = by_shard == shard * (kinds * 4) + kind * 4 + by_kind % 4
    return jnp.where(hit, 1.0, 0.0).astype(BF16)


def delayed(value):
    lane = lax.broadcasted_iota(jnp.int32, (ROWS, LANES), 1)
    row = lax.broadcasted_iota(jnp.int32, (ROWS, LANES), 0)
    above = jnp.where(row == 0, 0.0, pltpu.roll(value, 1, 0))
    return [
        pltpu.roll(jnp.where(lane >= LANES - steps, above, value), steps, 1) for steps in (1, 2)
    ]


def advanced(value):
    lane = lax.broadcasted_iota(jnp.int32, (ROWS, LANES), 1)
    row = lax.broadcasted_iota(jnp.int32, (ROWS, LANES), 0)
    below = jnp.where(row == ROWS - 1, 0.0, pltpu.roll(value, ROWS - 1, 0))
    return [pltpu.roll(jnp.where(lane < steps, below, value), LANES - steps, 1) for steps in (1, 2)]


def put_groups(target, rows):
    target[0:32] = rows[:, :LANES].astype(BF16).reshape(32, 8, LANES)
    target[32:64] = rows[:, LANES:].astype(BF16).reshape(32, 8, LANES)


def get_groups(source):
    return side_by_side(*[source[32 * m : 32 * (m + 1)].reshape(256, LANES) for m in range(2)])


def stack_groups(rows):
    return [
        jnp.concatenate([rows[at : at + 128, :LANES], rows[at : at + 128, LANES:]], axis=0)
        for at in (0, 128)
    ]


def side_by_side(left, right):
    return jnp.concatenate([left, right], axis=1)


def kernel(
    q_hbm, k_hbm, v_hbm, g_hbm, filt_hbm, qt_hbm, kt_hbm, vt_hbm, gain_hbm,
    first_hbm, last_hbm, mid_hbm, back_hbm, twist_hbm,
    recv_c, recv_d,
    q_ref, k_ref, v_ref, g_ref, filt_ref, qt_ref, kt_ref, vt_ref, gain_ref,
    first_ref, last_ref, mid_ref, back_ref, twist_ref,
    send_a, recv_a, send_b, recv_b, send_f, recv_f, send_c, send_d,
    filt_spec, short_k, short_v, mixed_ref, grad_ref,
    input_sem, taps_sem, table_sem,
    in_a_sem, in_b_sem, out_c_sem, out_d_sem,
    send_f_sem, recv_f_sem, share_send_sem, share_recv_sem,
):
    me = lax.axis_index("seq")
    group = lax.axis_index("chan")
    home, core = me % CHAN, group % 2
    at_home = home == group
    across = home == (group + 2) % CHAN
    direct = home % 2 == core
    channel = home * FILTERS + me // CHAN
    core_peer = group + 1 - 2 * core
    planes = [(me // 8 + dz) % 8 * 8 for dz in range(8)]
    highs = [(me // 4 + dx) % 2 * 4 for dx in range(2)]
    lows = [home, home + 1 - 2 * (me % 2), (home + 2) % 4, (home + 2) % 4 + 1 - 2 * (me % 2)]

    def hops(dz, high, low):
        return min(dz, 8 - dz) + (low // 2 if high == 0 else 2 - low // 2) + low % 2

    steps = [(dz, high, low) for low in range(4) for high in range(2) for dz in range(8)]
    steps = sorted(steps[1:], key=lambda step: -hops(*step))

    def copies(pairs, sems):
        return [
            pltpu.make_async_copy(source, target, sems.at[index])
            for index, (source, target) in enumerate(pairs)
        ]

    input_copies = copies(
        [(filt_hbm, filt_ref), (q_hbm, q_ref), (k_hbm, k_ref), (v_hbm, v_ref), (g_hbm, g_ref)],
        input_sem,
    )
    taps_copies = copies(
        [(qt_hbm, qt_ref), (kt_hbm, kt_ref), (vt_hbm, vt_ref), (gain_hbm, gain_ref)], taps_sem
    )
    table_copies = copies(
        [
            (first_hbm, first_ref),
            (mid_hbm, mid_ref),
            (twist_hbm, twist_ref),
            (back_hbm, back_ref),
            (last_hbm, last_ref),
        ],
        table_sem,
    )
    for copy in input_copies:
        copy.start()

    barrier = pltpu.get_barrier_semaphore()


    @pl.when(across)
    def _():
        for dz, high, low in steps + [(0, 0, 0)]:
            source = planes[dz] + highs[high] + lows[low]
            pl.semaphore_signal(
                barrier, inc=1, device_id={"seq": source, "chan": home}, device_id_type=MESH
            )

    for dz, high, low in steps:
        partner = planes[dz] + highs[high] + lows[low]
        pl.semaphore_signal(barrier, inc=1, device_id={"seq": partner}, device_id_type=MESH)
    pl.semaphore_signal(barrier, inc=1, device_id={"chan": core_peer}, device_id_type=MESH)
    for copy in taps_copies + table_copies:
        copy.start()
    input_copies[0].wait()

    filt_h, filt_l = split(filt_ref[...])
    pieces = [part[:, LANES * j : LANES * (j + 1)] for part in (filt_h, filt_l) for j in range(4)]
    row = lax.broadcasted_iota(jnp.int32, (128, 128), 0)
    col = lax.broadcasted_iota(jnp.int32, (128, 128), 1)
    regroup = jnp.where((row % 8 == col // 16) & (row // 8 == col % 16), 1.0, 0.0).astype(BF16)
    send_f[...] = dot(regroup, jnp.concatenate(pieces, axis=0)).astype(BF16).reshape(FILTERS, 8, LANES)
    swap = swap_matrix(32)
    for copy in input_copies[1:]:
        copy.wait()
    for target, refs in ((send_a, (k_ref, v_ref)), (send_b, (q_ref, g_ref))):
        groups = [
            jnp.concatenate(
                [
                    ref[32 * m : 32 * (m + 1), LANES * j : LANES * (j + 1)]
                    for ref in refs
                    for j in range(4)
                ],
                axis=0,
            )
            for m in range(2)
        ]
        put_groups(target, dot(swap, side_by_side(*groups)))

    pl.semaphore_wait(barrier, SEQ - 1 + FILTERS + 1)

    def send_filter(r, target_group):
        pltpu.make_async_remote_copy(
            src_ref=send_f.at[r],
            dst_ref=recv_f.at[me],
            send_sem=send_f_sem,
            recv_sem=recv_f_sem,
            device_id={"seq": CHAN * r + group, "chan": target_group},
            device_id_type=MESH,
        ).start()

    for step in sorted(range(FILTERS), key=lambda step: -min(step, FILTERS - step)):
        row = (me // CHAN + step) % FILTERS
        send_filter(row, (group + 2) % CHAN)
        if step > 0:
            send_filter(row, group)

    @pl.when(at_home)
    def _():
        pltpu.make_async_copy(send_f.at[me // CHAN], recv_f.at[me], recv_f_sem).start()

    @pl.when(jnp.logical_not(at_home))
    def _():
        send_filter(me // CHAN, group)

    def send_inputs(source, target, sems):
        pltpu.make_async_copy(source.at[channel], target.at[me], sems.at[1]).start()
        for dz, high, low in steps:
            place = planes[dz] + highs[high]
            pltpu.make_async_remote_copy(
                src_ref=source.at[lows[low] * FILTERS + place // CHAN],
                dst_ref=target.at[me],
                send_sem=sems.at[0],
                recv_sem=sems.at[1],
                device_id={"seq": place + lows[low]},
                device_id_type=MESH,
            ).start()

    def send_outputs(source, target, sems):
        pltpu.make_async_copy(source.at[me], target.at[channel], sems.at[1]).start()
        for dz, high, low in steps:
            place = planes[dz] + highs[high] + lows[low]
            pltpu.make_async_remote_copy(
                src_ref=source.at[place],
                dst_ref=target.at[channel],
                send_sem=sems.at[0],
                recv_sem=sems.at[1],
                device_id={"seq": place},
                device_id_type=MESH,
            ).start()

    send_inputs(send_a, recv_a, in_a_sem)
    send_inputs(send_b, recv_b, in_b_sem)

    @pl.when(direct)
    def _():
        pltpu.make_async_copy(recv_f, recv_f, recv_f_sem).wait()
        pltpu.make_async_remote_copy(
            src_ref=recv_f,
            dst_ref=recv_f,
            send_sem=share_send_sem,
            recv_sem=share_recv_sem,
            device_id={"chan": core_peer},
            device_id_type=MESH,
        ).start()

    for copy in taps_copies + table_copies:
        copy.wait()

    cosine, sine = twist_ref[0], twist_ref[1]

    def twist(real, imag):
        return side_by_side(real * cosine + imag * sine, imag * cosine - real * sine)

    def untwist(back):
        real, imag = back[:, :LANES], back[:, LANES:]
        return jnp.concatenate([real * cosine - imag * sine, imag * cosine + real * sine], axis=0)

    def short_filter(signal, taps, near, far):
        return taps[0, channel] * signal + taps[1, channel] * near + taps[2, channel] * far

    def causal_taps(signal, taps):
        return short_filter(signal, taps, *delayed(signal))

    def reverse_taps(signal, taps):
        return short_filter(signal, taps, *advanced(signal))

    sort_in = sort_matrix(32, 2, True)
    sort_out = sort_matrix(32, 2, False)
    gain = gain_ref[channel]

    pltpu.make_async_copy(recv_a, recv_a, in_a_sem.at[1]).wait()
    key, value = stack_groups(dot(sort_in, get_groups(recv_a)))
    short_k[...] = causal_taps(key, kt_ref)
    short_v[...] = causal_taps(value, vt_ref)
    product = short_k[...] * short_v[...]
    prod_h, prod_l = split(product)

    @pl.when(jnp.logical_not(direct))
    def _():
        pltpu.make_async_copy(recv_f, recv_f, share_recv_sem).wait()

    filt_h, filt_l = stack_groups(dot(sort_in, get_groups(recv_f)).astype(BF16))
    outer = table_left(first_ref, side_by_side(filt_h, prod_h), side_by_side(filt_l, prod_l))
    turned = jnp.concatenate(
        [
            twist(outer[:ROWS, :LANES], outer[ROWS:, :LANES]),
            twist(outer[:ROWS, LANES:], outer[ROWS:, LANES:]),
        ],
        axis=0,
    )
    spec = table_right(*split(turned), mid_ref)
    filt_re, filt_im = spec[:ROWS, :LANES], spec[:ROWS, LANES:]
    prod_re, prod_im = spec[ROWS:, :LANES], spec[ROWS:, LANES:]
    filt_spec[...] = spec[:ROWS]

    def inverse(real, imag):
        back = table_right(*split(side_by_side(real, imag)), back_ref)
        return table_left(last_ref, *split(untwist(back)))

    causal = inverse(filt_re * prod_re - filt_im * prod_im, filt_re * prod_im + filt_im * prod_re)
    mixed_ref[...] = causal + gain * product

    pltpu.make_async_copy(recv_b, recv_b, in_b_sem.at[1]).wait()
    query, cotangent = stack_groups(dot(sort_in, get_groups(recv_b)))
    short_q = causal_taps(query, qt_ref)
    mixed = mixed_ref[...]
    grad_ref[...] = cotangent * short_q

    def leave(target, first, second):
        first, second = first.astype(BF16), second.astype(BF16)
        groups = [
            jnp.concatenate([first[at : at + 128], second[at : at + 128]], axis=0)
            for at in (0, 128)
        ]
        put_groups(target, dot(sort_out, side_by_side(*groups)))

    leave(send_c, short_q * mixed, reverse_taps(cotangent * mixed, qt_ref))

    grad_mixed = grad_ref[...]
    outer = table_left(first_ref, *split(grad_mixed))
    spec = table_right(*split(twist(outer[:ROWS], outer[ROWS:])), mid_ref)
    grad_re, grad_im = spec[:, :LANES], spec[:, LANES:]
    filt_re, filt_im = filt_spec[:, :LANES], filt_spec[:, LANES:]
    send_outputs(send_c, recv_c, out_c_sem)
    backward = inverse(
        filt_re * grad_re + filt_im * grad_im, filt_re * grad_im - filt_im * grad_re
    )
    grad_product = backward + gain * grad_mixed
    leave(
        send_d,
        reverse_taps(grad_product * short_v[...], kt_ref),
        reverse_taps(grad_product * short_k[...], vt_ref),
    )
    send_outputs(send_d, recv_d, out_d_sem)

    for source, sems in (
        (send_a, in_a_sem), (send_b, in_b_sem), (send_c, out_c_sem), (send_d, out_d_sem)
    ):
        sent = source.at[pl.ds(0, SEQ - 1)]
        pltpu.make_async_copy(sent, sent, sems.at[0]).wait()
    pltpu.make_async_copy(send_f, send_f, send_f_sem).wait()

    @pl.when(at_home)
    def _():
        some = send_f.at[pl.ds(0, FILTERS - 1)]
        pltpu.make_async_copy(some, some, send_f_sem).wait()

    @pl.when(jnp.logical_not(at_home))
    def _():
        pltpu.make_async_copy(send_f, send_f, send_f_sem).wait()

    @pl.when(direct)
    def _():
        pltpu.make_async_copy(recv_f, recv_f, share_send_sem).wait()

    pltpu.make_async_copy(recv_c, recv_c, out_c_sem.at[1]).wait()
    pltpu.make_async_copy(recv_d, recv_d, out_d_sem.at[1]).wait()


def scatter_kernel(c_hbm, d_hbm, *refs):
    out_hbm, in_refs, out_refs, in_sem, out_sem = refs[:4], refs[4:6], refs[6:10], refs[10], refs[11]
    loads = [
        pltpu.make_async_copy(hbm, ref, in_sem.at[i])
        for i, (hbm, ref) in enumerate(zip((c_hbm, d_hbm), in_refs))
    ]
    for load in loads:
        load.start()
    swap = swap_matrix(8)
    stores = []
    for n in range(2):
        loads[n].wait()
        rows = dot(swap, get_groups(in_refs[n])).astype(BF16)
        for i in range(2):
            ref = out_refs[2 * n + i]
            for j in range(4):
                at = (4 * i + j) * 32
                for m in range(2):
                    ref[32 * m : 32 * (m + 1), LANES * j : LANES * (j + 1)] = rows[
                        at : at + 32, LANES * m : LANES * (m + 1)
                    ]
            stores.append(pltpu.make_async_copy(ref, out_hbm[2 * n + i], out_sem.at[2 * n + i]))
            stores[-1].start()
    for store in stores:
        store.wait()


def body(q, k, v, long_filter, q_taps, k_taps, v_taps, gain, cotangent):
    constants = [jnp.asarray(table) for table in tables()]
    hbm = pl.BlockSpec(memory_space=pltpu.HBM)
    block = pltpu.VMEM((SEQ, BLOCK), BF16)
    wave = pltpu.VMEM((SEQ, 8, LANES), BF16)
    signal = pltpu.VMEM((ROWS, LANES), F32)
    arrived = pl.pallas_call(
        kernel,
        out_shape=[jax.ShapeDtypeStruct((SEQ, 8, LANES), BF16)] * 2,
        in_specs=[hbm] * 14,
        out_specs=[hbm] * 2,
        scratch_shapes=[block] * 4
        + [pltpu.VMEM((FILTERS, BLOCK), F32)]
        + [pltpu.SMEM((3, SEQ), F32)] * 3
        + [pltpu.SMEM((SEQ,), F32)]
        + [
            pltpu.VMEM((2, 512, 256), BF16),
            pltpu.VMEM((2, 256, 512), BF16),
            pltpu.VMEM((2, 256, 256), BF16),
            pltpu.VMEM((2, 256, 256), BF16),
            pltpu.VMEM((2, ROWS, LANES), F32),
            wave,
            wave,
            wave,
            wave,
            pltpu.VMEM((FILTERS, 8, LANES), BF16),
            wave,
            wave,
            wave,
            pltpu.VMEM((ROWS, 2 * LANES), F32),
        ]
        + [signal] * 4
        + [
            pltpu.SemaphoreType.DMA((5,)),
            pltpu.SemaphoreType.DMA((4,)),
            pltpu.SemaphoreType.DMA((5,)),
        ]
        + [pltpu.SemaphoreType.DMA((2,))] * 4
        + [pltpu.SemaphoreType.DMA] * 4,
        compiler_params=pltpu.CompilerParams(
            collective_id=0, has_side_effects=True, vmem_limit_bytes=VMEM_LIMIT
        ),
        name="hyena",
    )(q, k, v, cotangent, long_filter, q_taps, k_taps, v_taps, gain, *constants)
    return pl.pallas_call(
        scatter_kernel,
        out_shape=[jax.ShapeDtypeStruct((SEQ, BLOCK), BF16)] * 4,
        in_specs=[hbm] * 2,
        out_specs=[hbm] * 4,
        scratch_shapes=[wave] * 2
        + [block] * 4
        + [pltpu.SemaphoreType.DMA((2,)), pltpu.SemaphoreType.DMA((4,))],
        compiler_params=pltpu.CompilerParams(vmem_limit_bytes=VMEM_LIMIT),
        name="scatter_rows",
    )(*arrived)


def solution(mesh):
    in_specs = (
        P("chan", "seq"),
        P("chan", "seq"),
        P("chan", "seq"),
        P("chan", "seq"),
        P(None, "chan"),
        P(None, "chan"),
        P(None, "chan"),
        P("chan"),
        P("chan", "seq"),
    )
    out_specs = (P("chan", "seq"),) * 4
    return jax.shard_map(body, mesh=mesh, in_specs=in_specs, out_specs=out_specs, check_vma=False)
```

```python
import functools

import jax
import jax.numpy as jnp
import ml_dtypes
import numpy as np
from jax import lax
from jax.experimental import pallas as pl
from jax.experimental.pallas import tpu as pltpu
from jax.sharding import PartitionSpec as P

SEQ = 64
CHAN = 4
BLOCK = 512
LANES = 128
ROWS = 256
FILTERS = SEQ // CHAN
FULL = 2 * ROWS * LANES
VMEM_LIMIT = 60 * 1024 * 1024

BF16 = jnp.bfloat16
F32 = jnp.float32
MESH = pl.DeviceIdType.MESH


def split_table(table):
    high = table.astype(ml_dtypes.bfloat16)
    low = (table - high.astype(np.float64)).astype(ml_dtypes.bfloat16)
    return high, low


@functools.lru_cache(maxsize=None)
def tables():
    k1 = np.arange(ROWS)
    a = np.arange(ROWS)
    b = np.arange(LANES)
    outer = 2 * np.pi * ((a[None, :] * (2 * k1[:, None] + 1)) % 1024) / 1024.0
    first = np.concatenate([np.cos(outer), -np.sin(outer)], axis=0)
    last = first.T * (2.0 / FULL)
    twist = 2 * np.pi * (b[None, :] * (2 * k1[:, None] + 1)) / (2.0 * FULL)
    inner = 2 * np.pi * ((b[None, :] * b[:, None]) % LANES) / LANES
    cosine, sine = np.cos(inner), np.sin(inner)
    mid = np.block([[cosine, -sine], [sine, cosine]])
    back = np.block([[cosine, sine], [-sine, cosine]])
    first_h, first_l = split_table(first)
    last_h, last_l = split_table(last)
    mid_h, mid_l = split_table(mid)
    back_h, back_l = split_table(back)
    return (
        np.stack([first_h, first_l]),
        np.stack([last_h, last_l]),
        np.stack([mid_h, mid_l]),
        np.stack([back_h, back_l]),
        np.stack([np.cos(twist), np.sin(twist)]).astype(np.float32),
    )


def split(value):
    high = value.astype(BF16)
    low = (value - high.astype(F32)).astype(BF16)
    return high, low


def dot(left, right):
    return jnp.dot(left, right, preferred_element_type=F32)


def table_left(table, high, low):
    table_h, table_l = table[0], table[1]
    left = jnp.concatenate([table_h, table_h, table_l], axis=1)
    return dot(left, jnp.concatenate([high, low, high], axis=0))


def table_right(high, low, table):
    table_h, table_l = table[0], table[1]
    right = jnp.concatenate([table_h, table_h, table_l], axis=0)
    return dot(jnp.concatenate([high, low, high], axis=1), right)


def swap_matrix(outer):
    row = lax.broadcasted_iota(jnp.int32, (256, 256), 0)
    col = lax.broadcasted_iota(jnp.int32, (256, 256), 1)
    inner = 256 // outer
    return jnp.where(col == row % inner * outer + row // inner, 1.0, 0.0).astype(BF16)


def sort_matrix(outer, kinds, to_kinds):
    size = outer * kinds * 4
    row = lax.broadcasted_iota(jnp.int32, (size, size), 0)
    col = lax.broadcasted_iota(jnp.int32, (size, size), 1)
    by_kind, by_shard = (row, col) if to_kinds else (col, row)
    kind = by_kind // (outer * 4)
    shard = (by_kind // 4) % outer
    hit = by_shard == shard * (kinds * 4) + kind * 4 + by_kind % 4
    return jnp.where(hit, 1.0, 0.0).astype(BF16)


def delayed(value):
    lane = lax.broadcasted_iota(jnp.int32, (ROWS, LANES), 1)
    row = lax.broadcasted_iota(jnp.int32, (ROWS, LANES), 0)
    above = jnp.where(row == 0, 0.0, pltpu.roll(value, 1, 0))
    return [
        pltpu.roll(jnp.where(lane >= LANES - steps, above, value), steps, 1) for steps in (1, 2)
    ]


def advanced(value):
    lane = lax.broadcasted_iota(jnp.int32, (ROWS, LANES), 1)
    row = lax.broadcasted_iota(jnp.int32, (ROWS, LANES), 0)
    below = jnp.where(row == ROWS - 1, 0.0, pltpu.roll(value, ROWS - 1, 0))
    return [pltpu.roll(jnp.where(lane < steps, below, value), LANES - steps, 1) for steps in (1, 2)]


def put_groups(target, rows):
    target[0:32] = rows[:, :LANES].astype(BF16).reshape(32, 8, LANES)
    target[32:64] = rows[:, LANES:].astype(BF16).reshape(32, 8, LANES)


def get_groups(source):
    return side_by_side(*[source[32 * m : 32 * (m + 1)].reshape(256, LANES) for m in range(2)])


def stack_groups(rows):
    return [
        jnp.concatenate([rows[at : at + 128, :LANES], rows[at : at + 128, LANES:]], axis=0)
        for at in (0, 128)
    ]


def side_by_side(left, right):
    return jnp.concatenate([left, right], axis=1)


def kernel(
    q_hbm, k_hbm, v_hbm, g_hbm, filt_hbm, qt_hbm, kt_hbm, vt_hbm, gain_hbm,
    first_hbm, last_hbm, mid_hbm, back_hbm, twist_hbm,
    recv_c, recv_d,
    q_ref, k_ref, v_ref, g_ref, filt_ref, qt_ref, kt_ref, vt_ref, gain_ref,
    first_ref, last_ref, mid_ref, back_ref, twist_ref,
    send_a, recv_a, send_b, recv_b, send_f, recv_f, send_c, send_d,
    filt_spec, short_k, short_v, mixed_ref, grad_ref,
    input_sem, taps_sem, table_sem,
    in_a_sem, in_b_sem, out_c_sem, out_d_sem,
    send_f_sem, recv_f_sem, share_send_sem, share_recv_sem,
):
    me = lax.axis_index("seq")
    group = lax.axis_index("chan")
    home, core = me % CHAN, group % 2
    at_home = home == group
    across = home == (group + 2) % CHAN
    direct = home % 2 == core
    channel = home * FILTERS + me // CHAN
    core_peer = group + 1 - 2 * core
    planes = [(me // 8 + dz) % 8 * 8 for dz in range(8)]
    highs = [(me // 4 + dx) % 2 * 4 for dx in range(2)]
    lows = [home, home + 1 - 2 * (me % 2), (home + 2) % 4, (home + 2) % 4 + 1 - 2 * (me % 2)]

    def hops(dz, high, low):
        return min(dz, 8 - dz) + (low // 2 if high == 0 else 2 - low // 2) + low % 2

    steps = [(dz, high, low) for low in range(4) for high in range(2) for dz in range(8)]
    steps = sorted(steps[1:], key=lambda step: -hops(*step))

    def copies(pairs, sems):
        return [
            pltpu.make_async_copy(source, target, sems.at[index])
            for index, (source, target) in enumerate(pairs)
        ]

    input_copies = copies(
        [(filt_hbm, filt_ref), (q_hbm, q_ref), (k_hbm, k_ref), (v_hbm, v_ref), (g_hbm, g_ref)],
        input_sem,
    )
    taps_copies = copies(
        [(qt_hbm, qt_ref), (kt_hbm, kt_ref), (vt_hbm, vt_ref), (gain_hbm, gain_ref)], taps_sem
    )
    table_copies = copies(
        [
            (first_hbm, first_ref),
            (mid_hbm, mid_ref),
            (twist_hbm, twist_ref),
            (back_hbm, back_ref),
            (last_hbm, last_ref),
        ],
        table_sem,
    )
    for copy in input_copies:
        copy.start()

    barrier = pltpu.get_barrier_semaphore()


    @pl.when(across)
    def _():
        for dz, high, low in steps + [(0, 0, 0)]:
            source = planes[dz] + highs[high] + lows[low]
            pl.semaphore_signal(
                barrier, inc=1, device_id={"seq": source, "chan": home}, device_id_type=MESH
            )
            if (dz, high, low) != (0, 0, 0):
                pl.semaphore_signal(
                    barrier, inc=1, device_id={"seq": source}, device_id_type=MESH
                )

    @pl.when(jnp.logical_not(across))
    def _():
        for dz, high, low in steps:
            partner = planes[dz] + highs[high] + lows[low]
            pl.semaphore_signal(barrier, inc=1, device_id={"seq": partner}, device_id_type=MESH)

    pl.semaphore_signal(barrier, inc=1, device_id={"chan": core_peer}, device_id_type=MESH)
    for copy in taps_copies + table_copies:
        copy.start()
    input_copies[0].wait()

    filt_h, filt_l = split(filt_ref[...])
    pieces = [part[:, LANES * j : LANES * (j + 1)] for part in (filt_h, filt_l) for j in range(4)]
    row = lax.broadcasted_iota(jnp.int32, (128, 128), 0)
    col = lax.broadcasted_iota(jnp.int32, (128, 128), 1)
    regroup = jnp.where((row % 8 == col // 16) & (row // 8 == col % 16), 1.0, 0.0).astype(BF16)
    send_f[...] = dot(regroup, jnp.concatenate(pieces, axis=0)).astype(BF16).reshape(FILTERS, 8, LANES)
    swap = swap_matrix(32)
    for copy in input_copies[1:]:
        copy.wait()
    for target, refs in ((send_a, (k_ref, v_ref)), (send_b, (q_ref, g_ref))):
        groups = [
            jnp.concatenate(
                [
                    ref[32 * m : 32 * (m + 1), LANES * j : LANES * (j + 1)]
                    for ref in refs
                    for j in range(4)
                ],
                axis=0,
            )
            for m in range(2)
        ]
        put_groups(target, dot(swap, side_by_side(*groups)))

    pl.semaphore_wait(barrier, SEQ - 1 + FILTERS + 1)

    def send_filter(r, target_group):
        pltpu.make_async_remote_copy(
            src_ref=send_f.at[r],
            dst_ref=recv_f.at[me],
            send_sem=send_f_sem,
            recv_sem=recv_f_sem,
            device_id={"seq": CHAN * r + group, "chan": target_group},
            device_id_type=MESH,
        ).start()

    for step in sorted(range(FILTERS), key=lambda step: -min(step, FILTERS - step)):
        row = (me // CHAN + step) % FILTERS
        send_filter(row, (group + 2) % CHAN)
        if step > 0:
            send_filter(row, group)

    @pl.when(at_home)
    def _():
        pltpu.make_async_copy(send_f.at[me // CHAN], recv_f.at[me], recv_f_sem).start()

    @pl.when(jnp.logical_not(at_home))
    def _():
        send_filter(me // CHAN, group)

    def send_inputs(source, target, sems):
        pltpu.make_async_copy(source.at[channel], target.at[me], sems.at[1]).start()
        for dz, high, low in steps:
            place = planes[dz] + highs[high]
            pltpu.make_async_remote_copy(
                src_ref=source.at[lows[low] * FILTERS + place // CHAN],
                dst_ref=target.at[me],
                send_sem=sems.at[0],
                recv_sem=sems.at[1],
                device_id={"seq": place + lows[low]},
                device_id_type=MESH,
            ).start()

    def send_outputs(source, target, sems):
        pltpu.make_async_copy(source.at[me], target.at[channel], sems.at[1]).start()
        for dz, high, low in steps:
            place = planes[dz] + highs[high] + lows[low]
            pltpu.make_async_remote_copy(
                src_ref=source.at[place],
                dst_ref=target.at[channel],
                send_sem=sems.at[0],
                recv_sem=sems.at[1],
                device_id={"seq": place},
                device_id_type=MESH,
            ).start()

    send_inputs(send_a, recv_a, in_a_sem)
    send_inputs(send_b, recv_b, in_b_sem)

    @pl.when(direct)
    def _():
        pltpu.make_async_copy(recv_f, recv_f, recv_f_sem).wait()
        pltpu.make_async_remote_copy(
            src_ref=recv_f,
            dst_ref=recv_f,
            send_sem=share_send_sem,
            recv_sem=share_recv_sem,
            device_id={"chan": core_peer},
            device_id_type=MESH,
        ).start()

    for copy in taps_copies + table_copies:
        copy.wait()

    cosine, sine = twist_ref[0], twist_ref[1]

    def twist(real, imag):
        return side_by_side(real * cosine + imag * sine, imag * cosine - real * sine)

    def untwist(back):
        real, imag = back[:, :LANES], back[:, LANES:]
        return jnp.concatenate([real * cosine - imag * sine, imag * cosine + real * sine], axis=0)

    def short_filter(signal, taps, near, far):
        return taps[0, channel] * signal + taps[1, channel] * near + taps[2, channel] * far

    def causal_taps(signal, taps):
        return short_filter(signal, taps, *delayed(signal))

    def reverse_taps(signal, taps):
        return short_filter(signal, taps, *advanced(signal))

    sort_in = sort_matrix(32, 2, True)
    sort_out = sort_matrix(32, 2, False)
    gain = gain_ref[channel]

    pltpu.make_async_copy(recv_a, recv_a, in_a_sem.at[1]).wait()
    key, value = stack_groups(dot(sort_in, get_groups(recv_a)))
    short_k[...] = causal_taps(key, kt_ref)
    short_v[...] = causal_taps(value, vt_ref)
    product = short_k[...] * short_v[...]
    prod_h, prod_l = split(product)

    @pl.when(jnp.logical_not(direct))
    def _():
        pltpu.make_async_copy(recv_f, recv_f, share_recv_sem).wait()

    filt_h, filt_l = stack_groups(dot(sort_in, get_groups(recv_f)).astype(BF16))
    outer = table_left(first_ref, side_by_side(filt_h, prod_h), side_by_side(filt_l, prod_l))
    turned = jnp.concatenate(
        [
            twist(outer[:ROWS, :LANES], outer[ROWS:, :LANES]),
            twist(outer[:ROWS, LANES:], outer[ROWS:, LANES:]),
        ],
        axis=0,
    )
    spec = table_right(*split(turned), mid_ref)
    filt_re, filt_im = spec[:ROWS, :LANES], spec[:ROWS, LANES:]
    prod_re, prod_im = spec[ROWS:, :LANES], spec[ROWS:, LANES:]
    filt_spec[...] = spec[:ROWS]

    def inverse(real, imag):
        back = table_right(*split(side_by_side(real, imag)), back_ref)
        return table_left(last_ref, *split(untwist(back)))

    causal = inverse(filt_re * prod_re - filt_im * prod_im, filt_re * prod_im + filt_im * prod_re)
    mixed_ref[...] = causal + gain * product

    pltpu.make_async_copy(recv_b, recv_b, in_b_sem.at[1]).wait()
    query, cotangent = stack_groups(dot(sort_in, get_groups(recv_b)))
    short_q = causal_taps(query, qt_ref)
    mixed = mixed_ref[...]
    grad_ref[...] = cotangent * short_q

    def leave(target, first, second):
        first, second = first.astype(BF16), second.astype(BF16)
        groups = [
            jnp.concatenate([first[at : at + 128], second[at : at + 128]], axis=0)
            for at in (0, 128)
        ]
        put_groups(target, dot(sort_out, side_by_side(*groups)))

    leave(send_c, short_q * mixed, reverse_taps(cotangent * mixed, qt_ref))

    grad_mixed = grad_ref[...]
    outer = table_left(first_ref, *split(grad_mixed))
    spec = table_right(*split(twist(outer[:ROWS], outer[ROWS:])), mid_ref)
    grad_re, grad_im = spec[:, :LANES], spec[:, LANES:]
    filt_re, filt_im = filt_spec[:, :LANES], filt_spec[:, LANES:]
    send_outputs(send_c, recv_c, out_c_sem)
    backward = inverse(
        filt_re * grad_re + filt_im * grad_im, filt_re * grad_im - filt_im * grad_re
    )
    grad_product = backward + gain * grad_mixed
    leave(
        send_d,
        reverse_taps(grad_product * short_v[...], kt_ref),
        reverse_taps(grad_product * short_k[...], vt_ref),
    )
    send_outputs(send_d, recv_d, out_d_sem)

    for source, sems in (
        (send_a, in_a_sem), (send_b, in_b_sem), (send_c, out_c_sem), (send_d, out_d_sem)
    ):
        sent = source.at[pl.ds(0, SEQ - 1)]
        pltpu.make_async_copy(sent, sent, sems.at[0]).wait()
    pltpu.make_async_copy(send_f, send_f, send_f_sem).wait()

    @pl.when(at_home)
    def _():
        some = send_f.at[pl.ds(0, FILTERS - 1)]
        pltpu.make_async_copy(some, some, send_f_sem).wait()

    @pl.when(jnp.logical_not(at_home))
    def _():
        pltpu.make_async_copy(send_f, send_f, send_f_sem).wait()

    @pl.when(direct)
    def _():
        pltpu.make_async_copy(recv_f, recv_f, share_send_sem).wait()

    pltpu.make_async_copy(recv_c, recv_c, out_c_sem.at[1]).wait()
    pltpu.make_async_copy(recv_d, recv_d, out_d_sem.at[1]).wait()


def scatter_kernel(c_hbm, d_hbm, *refs):
    out_hbm, in_refs, out_refs, in_sem, out_sem = refs[:4], refs[4:6], refs[6:10], refs[10], refs[11]
    loads = [
        pltpu.make_async_copy(hbm, ref, in_sem.at[i])
        for i, (hbm, ref) in enumerate(zip((c_hbm, d_hbm), in_refs))
    ]
    for load in loads:
        load.start()
    swap = swap_matrix(8)
    stores = []
    for n in range(2):
        loads[n].wait()
        rows = dot(swap, get_groups(in_refs[n])).astype(BF16)
        for i in range(2):
            ref = out_refs[2 * n + i]
            for j in range(4):
                at = (4 * i + j) * 32
                for m in range(2):
                    ref[32 * m : 32 * (m + 1), LANES * j : LANES * (j + 1)] = rows[
                        at : at + 32, LANES * m : LANES * (m + 1)
                    ]
            stores.append(pltpu.make_async_copy(ref, out_hbm[2 * n + i], out_sem.at[2 * n + i]))
            stores[-1].start()
    for store in stores:
        store.wait()


def body(q, k, v, long_filter, q_taps, k_taps, v_taps, gain, cotangent):
    constants = [jnp.asarray(table) for table in tables()]
    hbm = pl.BlockSpec(memory_space=pltpu.HBM)
    block = pltpu.VMEM((SEQ, BLOCK), BF16)
    wave = pltpu.VMEM((SEQ, 8, LANES), BF16)
    signal = pltpu.VMEM((ROWS, LANES), F32)
    arrived = pl.pallas_call(
        kernel,
        out_shape=[jax.ShapeDtypeStruct((SEQ, 8, LANES), BF16)] * 2,
        in_specs=[hbm] * 14,
        out_specs=[hbm] * 2,
        scratch_shapes=[block] * 4
        + [pltpu.VMEM((FILTERS, BLOCK), F32)]
        + [pltpu.SMEM((3, SEQ), F32)] * 3
        + [pltpu.SMEM((SEQ,), F32)]
        + [
            pltpu.VMEM((2, 512, 256), BF16),
            pltpu.VMEM((2, 256, 512), BF16),
            pltpu.VMEM((2, 256, 256), BF16),
            pltpu.VMEM((2, 256, 256), BF16),
            pltpu.VMEM((2, ROWS, LANES), F32),
            wave,
            wave,
            wave,
            wave,
            pltpu.VMEM((FILTERS, 8, LANES), BF16),
            wave,
            wave,
            wave,
            pltpu.VMEM((ROWS, 2 * LANES), F32),
        ]
        + [signal] * 4
        + [
            pltpu.SemaphoreType.DMA((5,)),
            pltpu.SemaphoreType.DMA((4,)),
            pltpu.SemaphoreType.DMA((5,)),
        ]
        + [pltpu.SemaphoreType.DMA((2,))] * 4
        + [pltpu.SemaphoreType.DMA] * 4,
        compiler_params=pltpu.CompilerParams(
            collective_id=0, has_side_effects=True, vmem_limit_bytes=VMEM_LIMIT
        ),
        name="hyena",
    )(q, k, v, cotangent, long_filter, q_taps, k_taps, v_taps, gain, *constants)
    return pl.pallas_call(
        scatter_kernel,
        out_shape=[jax.ShapeDtypeStruct((SEQ, BLOCK), BF16)] * 4,
        in_specs=[hbm] * 2,
        out_specs=[hbm] * 4,
        scratch_shapes=[wave] * 2
        + [block] * 4
        + [pltpu.SemaphoreType.DMA((2,)), pltpu.SemaphoreType.DMA((4,))],
        compiler_params=pltpu.CompilerParams(vmem_limit_bytes=VMEM_LIMIT),
        name="scatter_rows",
    )(*arrived)


def solution(mesh):
    in_specs = (
        P("chan", "seq"),
        P("chan", "seq"),
        P("chan", "seq"),
        P("chan", "seq"),
        P(None, "chan"),
        P(None, "chan"),
        P(None, "chan"),
        P("chan"),
        P("chan", "seq"),
    )
    out_specs = (P("chan", "seq"),) * 4
    return jax.shard_map(body, mesh=mesh, in_specs=in_specs, out_specs=out_specs, check_vma=False)
```

```python
import functools

import jax
import jax.numpy as jnp
import ml_dtypes
import numpy as np
from jax import lax
from jax.experimental import pallas as pl
from jax.experimental.pallas import tpu as pltpu
from jax.sharding import PartitionSpec as P

SEQ = 64
CHAN = 4
BLOCK = 512
LANES = 128
ROWS = 256
FILTERS = SEQ // CHAN
FULL = 2 * ROWS * LANES
VMEM_LIMIT = 60 * 1024 * 1024

BF16 = jnp.bfloat16
F32 = jnp.float32
MESH = pl.DeviceIdType.MESH


def split_table(table):
    high = table.astype(ml_dtypes.bfloat16)
    low = (table - high.astype(np.float64)).astype(ml_dtypes.bfloat16)
    return high, low


@functools.lru_cache(maxsize=None)
def tables():
    k1 = np.arange(ROWS)
    a = np.arange(ROWS)
    b = np.arange(LANES)
    outer = 2 * np.pi * ((a[None, :] * (2 * k1[:, None] + 1)) % 1024) / 1024.0
    first = np.concatenate([np.cos(outer), -np.sin(outer)], axis=0)
    last = first.T * (2.0 / FULL)
    twist = 2 * np.pi * (b[None, :] * (2 * k1[:, None] + 1)) / (2.0 * FULL)
    inner = 2 * np.pi * ((b[None, :] * b[:, None]) % LANES) / LANES
    cosine, sine = np.cos(inner), np.sin(inner)
    mid = np.block([[cosine, -sine], [sine, cosine]])
    back = np.block([[cosine, sine], [-sine, cosine]])
    first_h, first_l = split_table(first)
    last_h, last_l = split_table(last)
    mid_h, mid_l = split_table(mid)
    back_h, back_l = split_table(back)
    return (
        np.stack([first_h, first_l]),
        np.stack([last_h, last_l]),
        np.stack([mid_h, mid_l]),
        np.stack([back_h, back_l]),
        np.stack([np.cos(twist), np.sin(twist)]).astype(np.float32),
    )


def split(value):
    high = value.astype(BF16)
    low = (value - high.astype(F32)).astype(BF16)
    return high, low


def dot(left, right):
    return jnp.dot(left, right, preferred_element_type=F32)


def table_left(table, high, low):
    table_h, table_l = table[0], table[1]
    left = jnp.concatenate([table_h, table_h, table_l], axis=1)
    return dot(left, jnp.concatenate([high, low, high], axis=0))


def table_right(high, low, table):
    table_h, table_l = table[0], table[1]
    right = jnp.concatenate([table_h, table_h, table_l], axis=0)
    return dot(jnp.concatenate([high, low, high], axis=1), right)


def swap_matrix(outer):
    row = lax.broadcasted_iota(jnp.int32, (256, 256), 0)
    col = lax.broadcasted_iota(jnp.int32, (256, 256), 1)
    inner = 256 // outer
    return jnp.where(col == row % inner * outer + row // inner, 1.0, 0.0).astype(BF16)


def sort_matrix(outer, kinds, to_kinds):
    size = outer * kinds * 4
    row = lax.broadcasted_iota(jnp.int32, (size, size), 0)
    col = lax.broadcasted_iota(jnp.int32, (size, size), 1)
    by_kind, by_shard = (row, col) if to_kinds else (col, row)
    kind = by_kind // (outer * 4)
    shard = (by_kind // 4) % outer
    hit = by_shard == shard * (kinds * 4) + kind * 4 + by_kind % 4
    return jnp.where(hit, 1.0, 0.0).astype(BF16)


def delayed(value):
    lane = lax.broadcasted_iota(jnp.int32, (ROWS, LANES), 1)
    row = lax.broadcasted_iota(jnp.int32, (ROWS, LANES), 0)
    above = jnp.where(row == 0, 0.0, pltpu.roll(value, 1, 0))
    return [
        pltpu.roll(jnp.where(lane >= LANES - steps, above, value), steps, 1) for steps in (1, 2)
    ]


def advanced(value):
    lane = lax.broadcasted_iota(jnp.int32, (ROWS, LANES), 1)
    row = lax.broadcasted_iota(jnp.int32, (ROWS, LANES), 0)
    below = jnp.where(row == ROWS - 1, 0.0, pltpu.roll(value, ROWS - 1, 0))
    return [pltpu.roll(jnp.where(lane < steps, below, value), LANES - steps, 1) for steps in (1, 2)]


def put_groups(target, rows):
    target[0:32] = rows[:, :LANES].astype(BF16).reshape(32, 8, LANES)
    target[32:64] = rows[:, LANES:].astype(BF16).reshape(32, 8, LANES)


def get_groups(source):
    return side_by_side(*[source[32 * m : 32 * (m + 1)].reshape(256, LANES) for m in range(2)])


def stack_groups(rows):
    return [
        jnp.concatenate([rows[at : at + 128, :LANES], rows[at : at + 128, LANES:]], axis=0)
        for at in (0, 128)
    ]


def side_by_side(left, right):
    return jnp.concatenate([left, right], axis=1)


def kernel(
    q_hbm, k_hbm, v_hbm, g_hbm, filt_hbm, qt_hbm, kt_hbm, vt_hbm, gain_hbm,
    first_hbm, last_hbm, mid_hbm, back_hbm, twist_hbm,
    recv_c, recv_d,
    q_ref, k_ref, v_ref, g_ref, filt_ref, qt_ref, kt_ref, vt_ref, gain_ref,
    first_ref, last_ref, mid_ref, back_ref, twist_ref,
    send_a, recv_a, send_b, recv_b, send_f, recv_f, send_c, send_d,
    filt_spec, short_k, short_v, mixed_ref, grad_ref,
    input_sem, taps_sem, table_sem,
    in_a_sem, in_b_sem, out_c_sem, out_d_sem,
    send_f_sem, recv_f_sem, share_send_sem, share_recv_sem,
):
    me = lax.axis_index("seq")
    group = lax.axis_index("chan")
    home, core = me % CHAN, group % 2
    at_home = home == group
    across = home == (group + 2) % CHAN
    direct = home % 2 == core
    channel = home * FILTERS + me // CHAN
    core_peer = group + 1 - 2 * core
    turn = group % 2 * 6 + 1
    planes = [(me // 8 + dz * turn) % 8 * 8 for dz in range(8)]
    highs = [(me // 4 + dx) % 2 * 4 for dx in range(2)]
    lows = [home, home + 1 - 2 * (me % 2), (home + 2) % 4, (home + 2) % 4 + 1 - 2 * (me % 2)]

    def hops(dz, high, low):
        return min(dz, 8 - dz) + (low // 2 if high == 0 else 2 - low // 2) + low % 2

    steps = [(dz, high, low) for low in range(4) for high in range(2) for dz in range(8)]
    steps = sorted(steps[1:], key=lambda step: -hops(*step))

    def copies(pairs, sems):
        return [
            pltpu.make_async_copy(source, target, sems.at[index])
            for index, (source, target) in enumerate(pairs)
        ]

    input_copies = copies(
        [(filt_hbm, filt_ref), (q_hbm, q_ref), (k_hbm, k_ref), (v_hbm, v_ref), (g_hbm, g_ref)],
        input_sem,
    )
    taps_copies = copies(
        [(qt_hbm, qt_ref), (kt_hbm, kt_ref), (vt_hbm, vt_ref), (gain_hbm, gain_ref)], taps_sem
    )
    table_copies = copies(
        [
            (first_hbm, first_ref),
            (mid_hbm, mid_ref),
            (twist_hbm, twist_ref),
            (back_hbm, back_ref),
            (last_hbm, last_ref),
        ],
        table_sem,
    )
    for copy in input_copies:
        copy.start()

    barrier = pltpu.get_barrier_semaphore()


    @pl.when(across)
    def _():
        for dz, high, low in steps + [(0, 0, 0)]:
            source = planes[dz] + highs[high] + lows[low]
            pl.semaphore_signal(
                barrier, inc=1, device_id={"seq": source, "chan": home}, device_id_type=MESH
            )
            if (dz, high, low) != (0, 0, 0):
                pl.semaphore_signal(
                    barrier, inc=1, device_id={"seq": source}, device_id_type=MESH
                )

    @pl.when(jnp.logical_not(across))
    def _():
        for dz, high, low in steps:
            partner = planes[dz] + highs[high] + lows[low]
            pl.semaphore_signal(barrier, inc=1, device_id={"seq": partner}, device_id_type=MESH)

    pl.semaphore_signal(barrier, inc=1, device_id={"chan": core_peer}, device_id_type=MESH)
    for copy in taps_copies + table_copies:
        copy.start()
    input_copies[0].wait()

    filt_h, filt_l = split(filt_ref[...])
    pieces = [part[:, LANES * j : LANES * (j + 1)] for part in (filt_h, filt_l) for j in range(4)]
    row = lax.broadcasted_iota(jnp.int32, (128, 128), 0)
    col = lax.broadcasted_iota(jnp.int32, (128, 128), 1)
    regroup = jnp.where((row % 8 == col // 16) & (row // 8 == col % 16), 1.0, 0.0).astype(BF16)
    send_f[...] = dot(regroup, jnp.concatenate(pieces, axis=0)).astype(BF16).reshape(FILTERS, 8, LANES)
    swap = swap_matrix(32)
    for copy in input_copies[1:]:
        copy.wait()
    for target, refs in ((send_a, (k_ref, v_ref)), (send_b, (q_ref, g_ref))):
        groups = [
            jnp.concatenate(
                [
                    ref[32 * m : 32 * (m + 1), LANES * j : LANES * (j + 1)]
                    for ref in refs
                    for j in range(4)
                ],
                axis=0,
            )
            for m in range(2)
        ]
        put_groups(target, dot(swap, side_by_side(*groups)))

    pl.semaphore_wait(barrier, SEQ - 1 + FILTERS + 1)

    def send_filter(r, target_group):
        pltpu.make_async_remote_copy(
            src_ref=send_f.at[r],
            dst_ref=recv_f.at[me],
            send_sem=send_f_sem,
            recv_sem=recv_f_sem,
            device_id={"seq": CHAN * r + group, "chan": target_group},
            device_id_type=MESH,
        ).start()

    for step in sorted(range(FILTERS), key=lambda step: -min(step, FILTERS - step)):
        row = (me // CHAN + step) % FILTERS
        send_filter(row, (group + 2) % CHAN)
        if step > 0:
            send_filter(row, group)

    @pl.when(at_home)
    def _():
        pltpu.make_async_copy(send_f.at[me // CHAN], recv_f.at[me], recv_f_sem).start()

    @pl.when(jnp.logical_not(at_home))
    def _():
        send_filter(me // CHAN, group)

    def send_inputs(source, target, sems):
        pltpu.make_async_copy(source.at[channel], target.at[me], sems.at[1]).start()
        for dz, high, low in steps:
            place = planes[dz] + highs[high]
            pltpu.make_async_remote_copy(
                src_ref=source.at[lows[low] * FILTERS + place // CHAN],
                dst_ref=target.at[me],
                send_sem=sems.at[0],
                recv_sem=sems.at[1],
                device_id={"seq": place + lows[low]},
                device_id_type=MESH,
            ).start()

    def send_outputs(source, target, sems):
        pltpu.make_async_copy(source.at[me], target.at[channel], sems.at[1]).start()
        for dz, high, low in steps:
            place = planes[dz] + highs[high] + lows[low]
            pltpu.make_async_remote_copy(
                src_ref=source.at[place],
                dst_ref=target.at[channel],
                send_sem=sems.at[0],
                recv_sem=sems.at[1],
                device_id={"seq": place},
                device_id_type=MESH,
            ).start()

    send_inputs(send_a, recv_a, in_a_sem)
    send_inputs(send_b, recv_b, in_b_sem)

    @pl.when(direct)
    def _():
        pltpu.make_async_copy(recv_f, recv_f, recv_f_sem).wait()
        pltpu.make_async_remote_copy(
            src_ref=recv_f,
            dst_ref=recv_f,
            send_sem=share_send_sem,
            recv_sem=share_recv_sem,
            device_id={"chan": core_peer},
            device_id_type=MESH,
        ).start()

    for copy in taps_copies + table_copies:
        copy.wait()

    cosine, sine = twist_ref[0], twist_ref[1]

    def twist(real, imag):
        return side_by_side(real * cosine + imag * sine, imag * cosine - real * sine)

    def untwist(back):
        real, imag = back[:, :LANES], back[:, LANES:]
        return jnp.concatenate([real * cosine - imag * sine, imag * cosine + real * sine], axis=0)

    def short_filter(signal, taps, near, far):
        return taps[0, channel] * signal + taps[1, channel] * near + taps[2, channel] * far

    def causal_taps(signal, taps):
        return short_filter(signal, taps, *delayed(signal))

    def reverse_taps(signal, taps):
        return short_filter(signal, taps, *advanced(signal))

    sort_in = sort_matrix(32, 2, True)
    sort_out = sort_matrix(32, 2, False)
    gain = gain_ref[channel]

    pltpu.make_async_copy(recv_a, recv_a, in_a_sem.at[1]).wait()
    key, value = stack_groups(dot(sort_in, get_groups(recv_a)))
    short_k[...] = causal_taps(key, kt_ref)
    short_v[...] = causal_taps(value, vt_ref)
    product = short_k[...] * short_v[...]
    prod_h, prod_l = split(product)

    @pl.when(jnp.logical_not(direct))
    def _():
        pltpu.make_async_copy(recv_f, recv_f, share_recv_sem).wait()

    filt_h, filt_l = stack_groups(dot(sort_in, get_groups(recv_f)).astype(BF16))
    outer = table_left(first_ref, side_by_side(filt_h, prod_h), side_by_side(filt_l, prod_l))
    turned = jnp.concatenate(
        [
            twist(outer[:ROWS, :LANES], outer[ROWS:, :LANES]),
            twist(outer[:ROWS, LANES:], outer[ROWS:, LANES:]),
        ],
        axis=0,
    )
    spec = table_right(*split(turned), mid_ref)
    filt_re, filt_im = spec[:ROWS, :LANES], spec[:ROWS, LANES:]
    prod_re, prod_im = spec[ROWS:, :LANES], spec[ROWS:, LANES:]
    filt_spec[...] = spec[:ROWS]

    def inverse(real, imag):
        back = table_right(*split(side_by_side(real, imag)), back_ref)
        return table_left(last_ref, *split(untwist(back)))

    causal = inverse(filt_re * prod_re - filt_im * prod_im, filt_re * prod_im + filt_im * prod_re)
    mixed_ref[...] = causal + gain * product

    pltpu.make_async_copy(recv_b, recv_b, in_b_sem.at[1]).wait()
    query, cotangent = stack_groups(dot(sort_in, get_groups(recv_b)))
    short_q = causal_taps(query, qt_ref)
    mixed = mixed_ref[...]
    grad_ref[...] = cotangent * short_q

    def leave(target, first, second):
        first, second = first.astype(BF16), second.astype(BF16)
        groups = [
            jnp.concatenate([first[at : at + 128], second[at : at + 128]], axis=0)
            for at in (0, 128)
        ]
        put_groups(target, dot(sort_out, side_by_side(*groups)))

    leave(send_c, short_q * mixed, reverse_taps(cotangent * mixed, qt_ref))

    grad_mixed = grad_ref[...]
    outer = table_left(first_ref, *split(grad_mixed))
    spec = table_right(*split(twist(outer[:ROWS], outer[ROWS:])), mid_ref)
    grad_re, grad_im = spec[:, :LANES], spec[:, LANES:]
    filt_re, filt_im = filt_spec[:, :LANES], filt_spec[:, LANES:]
    send_outputs(send_c, recv_c, out_c_sem)
    backward = inverse(
        filt_re * grad_re + filt_im * grad_im, filt_re * grad_im - filt_im * grad_re
    )
    grad_product = backward + gain * grad_mixed
    leave(
        send_d,
        reverse_taps(grad_product * short_v[...], kt_ref),
        reverse_taps(grad_product * short_k[...], vt_ref),
    )
    send_outputs(send_d, recv_d, out_d_sem)

    for source, sems in (
        (send_a, in_a_sem), (send_b, in_b_sem), (send_c, out_c_sem), (send_d, out_d_sem)
    ):
        sent = source.at[pl.ds(0, SEQ - 1)]
        pltpu.make_async_copy(sent, sent, sems.at[0]).wait()
    pltpu.make_async_copy(send_f, send_f, send_f_sem).wait()

    @pl.when(at_home)
    def _():
        some = send_f.at[pl.ds(0, FILTERS - 1)]
        pltpu.make_async_copy(some, some, send_f_sem).wait()

    @pl.when(jnp.logical_not(at_home))
    def _():
        pltpu.make_async_copy(send_f, send_f, send_f_sem).wait()

    @pl.when(direct)
    def _():
        pltpu.make_async_copy(recv_f, recv_f, share_send_sem).wait()

    pltpu.make_async_copy(recv_c, recv_c, out_c_sem.at[1]).wait()
    pltpu.make_async_copy(recv_d, recv_d, out_d_sem.at[1]).wait()


def scatter_kernel(c_hbm, d_hbm, *refs):
    out_hbm, in_refs, out_refs, in_sem, out_sem = refs[:4], refs[4:6], refs[6:10], refs[10], refs[11]
    loads = [
        pltpu.make_async_copy(hbm, ref, in_sem.at[i])
        for i, (hbm, ref) in enumerate(zip((c_hbm, d_hbm), in_refs))
    ]
    for load in loads:
        load.start()
    swap = swap_matrix(8)
    stores = []
    for n in range(2):
        loads[n].wait()
        rows = dot(swap, get_groups(in_refs[n])).astype(BF16)
        for i in range(2):
            ref = out_refs[2 * n + i]
            for j in range(4):
                at = (4 * i + j) * 32
                for m in range(2):
                    ref[32 * m : 32 * (m + 1), LANES * j : LANES * (j + 1)] = rows[
                        at : at + 32, LANES * m : LANES * (m + 1)
                    ]
            stores.append(pltpu.make_async_copy(ref, out_hbm[2 * n + i], out_sem.at[2 * n + i]))
            stores[-1].start()
    for store in stores:
        store.wait()


def body(q, k, v, long_filter, q_taps, k_taps, v_taps, gain, cotangent):
    constants = [jnp.asarray(table) for table in tables()]
    hbm = pl.BlockSpec(memory_space=pltpu.HBM)
    block = pltpu.VMEM((SEQ, BLOCK), BF16)
    wave = pltpu.VMEM((SEQ, 8, LANES), BF16)
    signal = pltpu.VMEM((ROWS, LANES), F32)
    arrived = pl.pallas_call(
        kernel,
        out_shape=[jax.ShapeDtypeStruct((SEQ, 8, LANES), BF16)] * 2,
        in_specs=[hbm] * 14,
        out_specs=[hbm] * 2,
        scratch_shapes=[block] * 4
        + [pltpu.VMEM((FILTERS, BLOCK), F32)]
        + [pltpu.SMEM((3, SEQ), F32)] * 3
        + [pltpu.SMEM((SEQ,), F32)]
        + [
            pltpu.VMEM((2, 512, 256), BF16),
            pltpu.VMEM((2, 256, 512), BF16),
            pltpu.VMEM((2, 256, 256), BF16),
            pltpu.VMEM((2, 256, 256), BF16),
            pltpu.VMEM((2, ROWS, LANES), F32),
            wave,
            wave,
            wave,
            wave,
            pltpu.VMEM((FILTERS, 8, LANES), BF16),
            wave,
            wave,
            wave,
            pltpu.VMEM((ROWS, 2 * LANES), F32),
        ]
        + [signal] * 4
        + [
            pltpu.SemaphoreType.DMA((5,)),
            pltpu.SemaphoreType.DMA((4,)),
            pltpu.SemaphoreType.DMA((5,)),
        ]
        + [pltpu.SemaphoreType.DMA((2,))] * 4
        + [pltpu.SemaphoreType.DMA] * 4,
        compiler_params=pltpu.CompilerParams(
            collective_id=0, has_side_effects=True, vmem_limit_bytes=VMEM_LIMIT
        ),
        name="hyena",
    )(q, k, v, cotangent, long_filter, q_taps, k_taps, v_taps, gain, *constants)
    return pl.pallas_call(
        scatter_kernel,
        out_shape=[jax.ShapeDtypeStruct((SEQ, BLOCK), BF16)] * 4,
        in_specs=[hbm] * 2,
        out_specs=[hbm] * 4,
        scratch_shapes=[wave] * 2
        + [block] * 4
        + [pltpu.SemaphoreType.DMA((2,)), pltpu.SemaphoreType.DMA((4,))],
        compiler_params=pltpu.CompilerParams(vmem_limit_bytes=VMEM_LIMIT),
        name="scatter_rows",
    )(*arrived)


def solution(mesh):
    in_specs = (
        P("chan", "seq"),
        P("chan", "seq"),
        P("chan", "seq"),
        P("chan", "seq"),
        P(None, "chan"),
        P(None, "chan"),
        P(None, "chan"),
        P("chan"),
        P("chan", "seq"),
    )
    out_specs = (P("chan", "seq"),) * 4
    return jax.shard_map(body, mesh=mesh, in_specs=in_specs, out_specs=out_specs, check_vma=False)
```
